256 devices in a mesh: mem: 8 (over z_hi, x), reg: 32 (over y, z_lo, core).
Axes of the slice: x: 4, y: 4, z: 8 (z_hi: 2, z_lo: 4; z = z_hi * 4 + z_lo), core: 2. Of those that a mesh axis runs over, the one named last changes fastest.
Arguments:
- ensemble: bfloat16 [256, 8, 16384], P('mem', None, 'reg'), may hold values from -6 to 6
- conv_first: bfloat16 [2, 9, 8, 64], replicated, may hold values from -0.75 to 0.75
- bias_first: float32 [2, 64], replicated, may hold values from -3 to 3
- conv_second: bfloat16 [2, 9, 64, 8], replicated, may hold values from -0.25 to 0.25
- bias_second: float32 [2, 8], replicated, may hold values from -3 to 3
- observed_cell: int32 [64, 16, 32], P('reg', 'mem'), may hold values from 0 to 127
- observed_value: float32 [64, 16, 32], P('reg', 'mem'), may hold values from -8 to 8
- observed_precision: float32 [64, 16, 32], P('reg', 'mem'), may hold values from 0.25 to 4
Outputs:
- analysis: bfloat16 [256, 8, 16384], P('mem', None, 'reg')
The draws below stay inside these ranges and needn't reach their ends.
All inputs are finite; a program needn't handle non-finite values. Where the reference program divides by a largest or mean magnitude, that divisor is 1e-20 or more.
Results may differ from the reference program's by a relative error of at most 0.0079.
Values may be sent and summed in bfloat16 or wider, within the bound.
A program may use at most 64 MiB of HBM per device.

```python
import math
import jax
import jax.numpy as jnp
from jax import lax

K = 256
C = 8
HID = 64
PS = 4
PATCH = 128
NOBS = 32
FLOW = 2
ITERS = 4
W = 64
ROWS = 256
NPR = 64
NPC = 16
CELLS = 16384


def plant(values, own_key, least, high):
    dims = values.shape
    spot = [jax.random.randint(jax.random.fold_in(own_key, axis), (), 0, dims[axis]) for axis in range(len(dims))]
    values = values.at[tuple(spot)].set(least)
    longest = dims.index(max(dims))
    spot[longest] = (spot[longest] + 1) % dims[longest]
    return values.at[tuple(spot)].set(high)


def block_scale(own_key, shape, cuts, least, top_value):
    loudness = 1.0
    for position, blocks in cuts:
        heights = jax.random.uniform(jax.random.fold_in(jax.random.fold_in(own_key, 6), position), (blocks,), jnp.float32, least / len(cuts), top_value / len(cuts))
        loudness = loudness * jnp.repeat(jnp.exp(heights), shape[position] // blocks).reshape((-1,) + (1,) * (len(shape) - 1 - position))
    return loudness


def bell_draw(rng, shape, scale, reach, pieces=(), kind=jnp.bfloat16):
    values = scale * jax.random.normal(rng, shape, jnp.float32)
    if pieces:
        values = values * block_scale(rng, shape, pieces, -0.22, 0.18)
    return jnp.clip(values, -reach, reach).astype(kind)


def setup_inputs(seed: int = 0) -> dict:
    keys = jax.random.split(jax.random.key(seed), 9)
    return {
        "ensemble": bell_draw(keys[0], (K, C, CELLS), 1.0, 6.0, ((0, 8), (2, 32))),
        "conv_first": bell_draw(keys[1], (FLOW, 9, C, HID), (9 * C) ** -0.5, 0.75),
        "bias_first": bell_draw(keys[2], (FLOW, HID), 0.5, 3.0, (), jnp.float32),
        "conv_second": bell_draw(keys[3], (FLOW, 9, HID, C), (9 * HID) ** -0.5, 0.25),
        "bias_second": bell_draw(keys[4], (FLOW, C), 0.5, 3.0, (), jnp.float32),
        "observed_cell": plant(jax.random.randint(keys[5], (NPR, NPC, NOBS), 0, PATCH), jax.random.fold_in(keys[5], 1), 0, PATCH - 1).astype(jnp.int32),
        "observed_value": bell_draw(keys[6], (NPR, NPC, NOBS), 1.5, 8.0, ((0, 32), (1, 8)), jnp.float32),
        "observed_precision": jnp.clip(jnp.exp(math.log(4.0) - 2.7725887 * jax.random.uniform(keys[7], (NPR, NPC, NOBS), jnp.float32) ** block_scale(keys[7], (NPR, NPC, NOBS), ((0, 32), (1, 8)), -0.2, 0.2)), 0.25, 4.0),
    }


PRECISE = lax.Precision.HIGHEST

def flow_block(zfield, conv_a, bias_a, conv_b, bias_b):
    kernel_a = jnp.transpose(conv_a.astype(jnp.float32).reshape(3, 3, C, HID), (3, 2, 0, 1))
    kernel_b = jnp.transpose(conv_b.astype(jnp.float32).reshape(3, 3, HID, C), (3, 2, 0, 1))
    numbers = ('NCHW', 'OIHW', 'NCHW')
    pre = lax.conv_general_dilated(zfield.astype(jnp.float32), kernel_a, (1, 1), ((1, 1), (1, 1)), dimension_numbers=numbers, precision=PRECISE)
    hidden = jax.nn.silu(pre + bias_a[None, :, None, None]).astype(jnp.bfloat16)
    branch = lax.conv_general_dilated(hidden.astype(jnp.float32), kernel_b, (1, 1), ((1, 1), (1, 1)), dimension_numbers=numbers, precision=PRECISE)
    return (zfield.astype(jnp.float32) + branch + bias_b[None, :, None, None]).astype(jnp.bfloat16)

def solve_weights(gram, summed):
    identity = jnp.eye(K, dtype=jnp.float32)
    system = gram + (K - 1) * identity
    bound = lax.optimization_barrier(jnp.max(lax.optimization_barrier(jnp.sum(jnp.abs(system), axis=-1)), axis=-1))
    iterate_y = system / bound[..., None, None]
    iterate_z = jnp.broadcast_to(identity, system.shape)
    for sweep in range(ITERS):
        turn = 1.5 * identity - 0.5 * jnp.matmul(iterate_z, iterate_y, precision=PRECISE)
        if sweep + 1 < ITERS:
            iterate_y = jnp.matmul(iterate_y, turn, precision=PRECISE)
        iterate_z = jnp.matmul(turn, iterate_z, precision=PRECISE)
    inner = jnp.einsum('...ij,...j->...i', iterate_z, summed, precision=PRECISE)
    mean_w = jnp.einsum('...ij,...j->...i', iterate_z, inner, precision=PRECISE) / bound[..., None]
    return jnp.sqrt((K - 1) / bound)[..., None, None] * iterate_z + mean_w[..., :, None]

def reference(ensemble, conv_first, bias_first, conv_second, bias_second, observed_cell, observed_value, observed_precision):
    grid = ensemble.reshape(K // 16, 16, C, ROWS, W)

    def run_flow(group):
        zfield = group
        for block in range(FLOW):
            zfield = flow_block(zfield, conv_first[block], bias_first[block], conv_second[block], bias_second[block])
        return zfield
    latent = lax.map(run_flow, grid).reshape(K, C, ROWS, W)
    tiles = latent.reshape(K, C, NPR, PS, NPC, PS).transpose(0, 2, 4, 1, 3, 5).reshape(K, NPR, NPC, PATCH)
    full = tiles.astype(jnp.float32)
    center = lax.optimization_barrier(jnp.mean(full, axis=0))
    spread = full - center
    cells = observed_cell.astype(jnp.int32)
    index = jnp.broadcast_to(cells[None], (K, NPR, NPC, NOBS)).astype(jnp.int32)
    seen = jnp.transpose(jnp.take_along_axis(spread, index, axis=3), (1, 2, 3, 0))
    seen_center = jnp.take_along_axis(center, cells, axis=2)
    root = jnp.sqrt(observed_precision)
    scaled = (seen * root[..., None]).astype(jnp.bfloat16)
    depart = (observed_value - seen_center) * root
    pulled = jnp.einsum('pqok,pqo->pqk', scaled.astype(jnp.float32), depart, precision=PRECISE).astype(jnp.bfloat16)
    padded_s = jnp.pad(scaled, ((2, 2), (2, 2), (0, 0), (0, 0)))
    padded_u = jnp.pad(pulled, ((2, 2), (2, 2), (0, 0)))

    def row_weights(row):
        blocks = []
        summed = jnp.zeros((NPC, K), jnp.float32)
        for row_step in range(-2, 3):
            start = (row + 2 + row_step).astype(jnp.int32)
            band_s = lax.dynamic_slice_in_dim(padded_s, start, 1, 0)[0]
            band_u = lax.dynamic_slice_in_dim(padded_u, start, 1, 0)[0]
            for col_step in range(-2, 3):
                dist = row_step ** 2 + col_step ** 2
                piece = band_s[2 + col_step:2 + col_step + NPC]
                blocks.append((piece.astype(jnp.float32) * math.exp(-dist / 9.0)).astype(jnp.bfloat16))
                summed = summed + band_u[2 + col_step:2 + col_step + NPC].astype(jnp.float32) * math.exp(-dist / 4.5)
        local = jnp.concatenate(blocks, axis=1).astype(jnp.float32)
        gram = jnp.einsum('qok,qol->qkl', local, local, precision=PRECISE)
        return solve_weights(gram, summed)
    weights = lax.map(row_weights, jnp.arange(NPR, dtype=jnp.int32))
    analysis = center + jnp.einsum('kpqv,pqkl->lpqv', spread, weights, precision=PRECISE)
    result = analysis.astype(jnp.bfloat16)
    return result.reshape(K, NPR, NPC, C, PS, PS).transpose(0, 3, 1, 4, 2, 5).reshape(K, C, ROWS * W)
```

```python
import functools

import jax
import jax.numpy as jnp
from jax import lax
from jax.experimental import pallas as pl
from jax.experimental.pallas import tpu as pltpu
from jax.sharding import PartitionSpec as P

K = 256
C = 8
HID = 64
NMEM = 8
NREG = 32
MEM_DEV = 32
NPC = 16
BF = jnp.bfloat16
F32 = jnp.float32
NEAR = [(dr, dm) for dr in (-1, 0, 1) for dm in (-1, 0, 1)]
TOP, BOTTOM = 4, 5


def dot(a, b):
    return lax.dot_general(a, b, (((1,), (0,)), ((), ())), preferred_element_type=F32)


def dot_nt(a, b):
    return lax.dot_general(a, b, (((1,), (1,)), ((), ())), preferred_element_type=F32)


def iota(shape, dim):
    return lax.broadcasted_iota(jnp.int32, shape, dim)


def block_swap(arrays):
    block = iota(arrays[0].shape, 1) // 16
    for step in (1, 2, 4):
        high = (block & step) != 0
        swapped = list(arrays)
        for a in range(8):
            if a & step:
                continue
            b = a | step
            swapped[a] = jnp.where(high, pltpu.roll(arrays[b], 16 * step, 1), arrays[a])
            swapped[b] = jnp.where(high, arrays[b], pltpu.roll(arrays[a], 128 - 16 * step, 1))
        arrays = swapped
    return arrays


def cell_order(inverse):
    plain, tiled = iota((256, 256), 1 if inverse else 0), iota((256, 256), 0 if inverse else 1)
    source = ((tiled // 4) % 4) * 64 + (tiled // 16) * 4 + tiled % 4
    return jnp.where(plain == source, 1.0, 0.0).astype(BF)


def strips_of(taps, flip):
    zero = jnp.zeros((C, HID), F32)
    strips = {}
    for row_step in (-1, 0, 1):
        for col in range(-1, 5):
            pieces = []
            for j in range(4):
                step = j - col if flip else col - j
                pieces.append(taps[3 * (row_step + 1) + step + 1] if abs(step) <= 1 else zero)
            strips[row_step, col] = jnp.concatenate(pieces, axis=1)
    return strips


def build_weights(taps, flip, raw, base):
    strips = strips_of(taps, flip)
    for tile in range(6):
        for row in range(4):
            if flip:
                hidden_row = {TOP: -1, BOTTOM: 4}.get(tile, tile)
                step = hidden_row - row
            else:
                step = {TOP: row - 4, BOTTOM: row + 4 - 3}.get(tile, row - tile)
            if abs(step) > 1:
                continue
            for side in (0, 1):
                for j in range(4):
                    col = j
                    if side:
                        col = {0: 4, 3: -1}.get(j)
                    if col is None:
                        continue
                    rows = pl.ds(4 * row + j, C, stride=16)
                    raw[base + tile, side, 0, rows, :] = strips[step, col][:, 0:128]
                    raw[base + tile, side, 1, rows, :] = strips[step, col][:, 128:256]


def kernel(
    ens_ref,
    first_ref,
    bias_a_ref,
    second_ref,
    bias_b_ref,
    cell_ref,
    value_ref,
    prec_ref,
    out_ref,
    raw,
    w_a,
    w_b,
    field,
    wide,
    hid,
    rel,
    rel_b,
    send_tiles,
    members,
    near,
    local,
    decay,
    send_back,
    back,
    halo_send,
    halo_recv,
    tile_send,
    tile_recv,
    near_send,
    near_recv,
    back_send,
    back_recv,
):
    m = lax.axis_index("mem")
    r = lax.axis_index("reg")
    barrier = pltpu.get_barrier_semaphore()

    def inside(dr, dm):
        return (r + dr >= 0) & (r + dr < NREG) & (m + dm >= 0) & (m + dm < NMEM)

    def peer(d):
        return lax.rem(m + d, NMEM)

    for d in range(1, NMEM):
        pl.semaphore_signal(
            barrier, inc=1, device_id={"mem": peer(d), "reg": r}, device_id_type=pl.DeviceIdType.MESH
        )
    arrivals = jnp.int32(NMEM - 1)
    for dr, dm in NEAR:
        if dr == 0:
            continue

        @pl.when(inside(dr, dm))
        def _(dr=dr, dm=dm):
            pl.semaphore_signal(
                barrier,
                inc=1,
                device_id={"mem": m + dm, "reg": r + dr},
                device_id_type=pl.DeviceIdType.MESH,
            )

        arrivals = arrivals + jnp.where(inside(dr, dm), 1, 0)

    order = cell_order(False)
    for p in range(2):
        cells = dot(ens_ref[:, 256 * p : 256 * p + 256], order)
        rel[0] = cells[:, 0:128]
        rel[1] = cells[:, 128:256]
        for half in range(2):
            channels = [rel[half, pl.ds(c, MEM_DEV, stride=C), :] for c in range(C)]
            for q, tile in enumerate(block_swap(channels)):
                field[0, 1 + p, 1 + 8 * half + q] = tile.astype(BF)
    edge = jnp.zeros((MEM_DEV, 128), BF)
    for f in range(2):
        for p in range(4):
            field[f, p, 0] = edge
            field[f, p, NPC + 1] = edge

    @pl.when(r == 0)
    def _():
        field[0, 0, 1 : NPC + 1] = jnp.zeros((NPC, MEM_DEV, 128), BF)

    @pl.when(r == NREG - 1)
    def _():
        field[0, 3, 1 : NPC + 1] = jnp.zeros((NPC, MEM_DEV, 128), BF)

    for slot, (dr, dm) in enumerate(NEAR):
        if (dr, dm) == (0, 0):
            continue

        @pl.when(jnp.logical_not(inside(dr, dm)))
        def _(slot=slot):
            near[slot] = jnp.zeros((K + 16, 128), BF)

    pl.semaphore_wait(barrier, arrivals)

    def halo_copy(down):
        return pltpu.make_async_remote_copy(
            src_ref=field.at[0, 2 if down else 1, pl.ds(1, NPC)],
            dst_ref=field.at[0, 0 if down else 3, pl.ds(1, NPC)],
            send_sem=halo_send.at[1 if down else 0],
            recv_sem=halo_recv.at[1 if down else 0],
            device_id={"mem": m, "reg": r + 1 if down else r - 1},
            device_id_type=pl.DeviceIdType.MESH,
        )

    @pl.when(r < NREG - 1)
    def _():
        halo_copy(True).start()

    @pl.when(r > 0)
    def _():
        halo_copy(False).start()

    raw[...] = jnp.zeros(raw.shape, F32)
    unit = jnp.where(iota((C, C), 0) == iota((C, C), 1), 1.0, 0.0).astype(BF)
    for f in range(2):
        taps = [
            0.5 * first_ref[pl.ds((9 * f + t) * C, C), :].astype(F32) for t in range(9)
        ]
        build_weights(taps, False, raw, 12 * f)
        turned = dot_nt(unit, second_ref[pl.ds(9 * HID * f, 9 * HID), :])
        taps = [turned[:, HID * t : HID * t + HID] for t in range(9)]
        build_weights(taps, True, raw, 12 * f + 6)
        for tile in range(6):
            for side in range(2):
                span = slice(128 * side, 128 * side + 128)
                for part in range(2):
                    lanes = slice(128 * part, 128 * part + 128)
                    w_a[f, tile, span, lanes] = raw[12 * f + tile, side, part].astype(BF)
                    w_b[f, tile, lanes, span] = jnp.transpose(
                        raw[12 * f + 6 + tile, side, part]
                    ).astype(BF)

    lane = iota((1, 128), 1)
    for target in range(4):
        for slot, (dr, dm) in enumerate(NEAR):
            a = 2 * dr + lane // 64 - target // 2
            b = 2 * dm + (lane // 32) % 2 - target % 2
            keep = (jnp.abs(a) <= 2) & (jnp.abs(b) <= 2) & inside(dr, dm)
            fall = jnp.exp((a * a + b * b).astype(F32) * (-1.0 / 9.0))
            decay[target, slot : slot + 1, :] = jnp.where(keep, fall, 0.0)

    row_lane = iota((1, 1, 128), 2)
    bias_lane = iota((1, 128), 1)
    keep_top = jnp.where(r == 0, 0.0, 1.0).astype(F32)
    keep_bottom = jnp.where(r == NREG - 1, 0.0, 1.0).astype(F32)
    keep = (keep_top, None, None, keep_bottom)

    def widen(f, p):
        right = field[f, p, 2 : NPC + 2].astype(F32)
        left = field[f, p, 0:NPC].astype(F32)
        side = jnp.where(row_lane % 4 < 2, right, left).astype(BF)
        wide[p, :, 0:128] = field[f, p, 1 : NPC + 1].reshape(NPC * MEM_DEV, 128)
        wide[p, :, 128:256] = side.reshape(NPC * MEM_DEV, 128)

    def hidden(f, p, i, bias):
        total = dot(wide[p], w_a[f, i])
        if i == 0:
            total = total + dot(wide[p - 1], w_a[f, TOP])
        if i == 3:
            total = total + dot(wide[p + 1], w_a[f, BOTTOM])
        total = total + bias
        total = total + total * jnp.tanh(total)
        if keep[p] is not None:
            total = total * keep[p]
        hid[p, i] = total.astype(BF)

    def branch(f, p, bias):
        total = None
        terms = [(p, i, i) for i in range(4)] + [(p - 1, 3, TOP), (p + 1, 0, BOTTOM)]
        if p == 0:
            terms = [(0, 1, 1), (0, 2, 2), (0, 3, 3), (1, 0, BOTTOM)]
        if p == 3:
            terms = [(3, 0, 0), (3, 1, 1), (3, 2, 2), (2, 3, TOP)]
        for hp, hi, tile in terms:
            part = dot(hid[hp, hi], w_b[f, tile])
            total = part if total is None else total + part
        own = total[:, 0:128].reshape(NPC, MEM_DEV, 128)
        side = total[:, 128:256].reshape(NPC, MEM_DEV, 128)
        none = jnp.zeros((1, MEM_DEV, 128), F32)
        before = jnp.concatenate([none, side[: NPC - 1]], axis=0)
        after = jnp.concatenate([side[1:], none], axis=0)
        moved = jnp.where(row_lane % 4 < 2, before, after)
        result = field[f, p, 1 : NPC + 1].astype(F32) + (own + moved + bias[None])
        if keep[p] is not None:
            result = result * keep[p]
        return result.astype(BF)

    def biases(f):
        half = 0.5 * bias_a_ref[f : f + 1, :]
        first = jnp.concatenate([half] * 4, axis=1)
        second = jnp.zeros((1, 128), F32)
        for c in range(C):
            second = jnp.where(bias_lane // 16 == c, bias_b_ref[f : f + 1, c : c + 1], second)
        return first, second

    bias_a, bias_b = biases(0)
    widen(0, 1)
    widen(0, 2)
    for p, i in ((1, 1), (1, 2), (2, 1), (2, 2), (1, 3), (2, 0)):
        hidden(0, p, i, bias_a)

    @pl.when(r < NREG - 1)
    def _():
        halo_copy(False).wait_recv()

    @pl.when(r > 0)
    def _():
        halo_copy(True).wait_recv()

    widen(0, 0)
    widen(0, 3)
    for p, i in ((1, 0), (2, 3), (0, 1), (0, 2), (0, 3), (3, 0), (3, 1), (3, 2)):
        hidden(0, p, i, bias_a)
    for p in range(4):
        field[1, p, 1 : NPC + 1] = branch(0, p, bias_b)

    bias_a, bias_b = biases(1)
    for p in range(4):
        widen(1, p)
    hidden(1, 0, 3, bias_a)
    hidden(1, 3, 0, bias_a)
    for p in (1, 2):
        for i in range(4):
            hidden(1, p, i, bias_a)
    for p in (1, 2):
        tiles = branch(1, p, bias_b).reshape(NMEM, 2, MEM_DEV, 128)
        for ql in range(2):
            send_tiles[:, 2 * (p - 1) + ql] = tiles[:, ql]

    def exchange(d, source, target, send_sem, recv_sem):
        return pltpu.make_async_remote_copy(
            src_ref=source.at[peer(d)],
            dst_ref=target.at[m],
            send_sem=send_sem.at[d],
            recv_sem=recv_sem.at[d],
            device_id={"mem": peer(d), "reg": r},
            device_id_type=pl.DeviceIdType.MESH,
        )

    tile_copies = [exchange(d, send_tiles, members, tile_send, tile_recv) for d in range(1, NMEM)]
    for copy in tile_copies:
        copy.start()
    members[m] = send_tiles[m]
    for copy in tile_copies:
        copy.wait_recv()

    def row_of(ref):
        return jnp.concatenate([ref[t // 2, t % 2 : t % 2 + 1, :] for t in range(4)], axis=1)

    cells = row_of(cell_ref)
    root = jnp.sqrt(row_of(prec_ref))
    picker = jnp.where(iota((128, 128), 0) == cells, 1.0, 0.0).astype(BF)
    seen = jnp.zeros((K, 128), F32)
    for t in range(4):
        tile = members[:, t].reshape(K, 128)
        seen = jnp.where(lane // 32 == t, dot(tile, picker), seen)
    seen_center = jnp.sum(seen, axis=0, keepdims=True) * (1.0 / K)
    near[4, 0:K] = ((seen - seen_center) * root).astype(BF)
    depart = (row_of(value_ref) - seen_center) * root
    depart_high = depart.astype(BF).astype(F32)
    depart_low = depart - depart_high
    sub = iota((16, 128), 0)
    near[4, K : K + 16] = jnp.where(
        sub == 0, depart_high, jnp.where(sub == 1, depart_low, 0.0)
    ).astype(BF)

    def near_copy(slot):
        dr, dm = NEAR[slot]
        return pltpu.make_async_remote_copy(
            src_ref=near.at[4],
            dst_ref=near.at[8 - slot],
            send_sem=near_send.at[slot],
            recv_sem=near_recv.at[8 - slot],
            device_id={"mem": m + dm, "reg": r + dr},
            device_id_type=pl.DeviceIdType.MESH,
        )

    for slot, (dr, dm) in enumerate(NEAR):
        if slot == 4:
            continue

        @pl.when(inside(dr, dm))
        def _(slot=slot):
            near_copy(slot).start()

    centers = []
    for t in range(4):
        tile = members[:, t].reshape(K, 128).astype(F32)
        centers.append(jnp.sum(tile, axis=0, keepdims=True) * (1.0 / K))

    for slot, (dr, dm) in enumerate(NEAR):
        if slot == 4:
            continue

        @pl.when(inside(dr, dm))
        def _(slot=slot):
            near_copy(8 - slot).wait_recv()

    summed = jnp.zeros((K, 8), F32)
    for slot in range(9):
        block = near[slot, 0:K].astype(F32)
        tail = near[slot, K : K + 16].astype(F32)
        depart = tail[0:1] + tail[1:2]
        pulls = []
        for t in range(4):
            fall = decay[t, slot : slot + 1, :]
            local[t, :, 128 * slot : 128 * slot + 128] = (block * fall).astype(BF)
            pulls.append(fall * fall * depart)
        pulls = jnp.concatenate(pulls, axis=0)
        high = pulls.astype(BF).astype(F32)
        both = jnp.concatenate([high, pulls - high], axis=0).astype(BF)
        summed = summed + dot_nt(near[slot, 0:K], both)

    eye = iota((K, K), 0) == iota((K, K), 1)
    for t in range(4):
        system = dot_nt(local[t], local[t]) + jnp.where(eye, float(K - 1), 0.0)
        rows = jnp.sum(jnp.abs(system), axis=0, keepdims=True)
        bound = jnp.max(rows, axis=1, keepdims=True)
        scale = 1.0 / bound
        a_mat = system * scale
        a_bf = a_mat.astype(BF)
        y = 1.5 * a_mat - 0.5 * dot(a_bf, a_bf)
        c = 1.5
        d_mat = -0.5 * a_mat
        for _ in range(2):
            y_bf = y.astype(BF)
            d_bf = d_mat.astype(BF)
            m_mat = c * y + dot(d_bf, y_bf)
            m_bf = m_mat.astype(BF)
            y = 1.5 * y - 0.5 * dot(y_bf, m_bf)
            d_mat = 1.5 * d_mat - (0.5 * c) * m_mat - 0.5 * dot(m_bf, d_bf)
            c = 1.5 * c
        y_bf = y.astype(BF)
        d_bf = d_mat.astype(BF)
        spread = members[:, t].reshape(K, 128).astype(F32) - centers[t]
        pull = summed[:, t : t + 1] + summed[:, 4 + t : 5 + t]
        x = jnp.concatenate([spread, jnp.broadcast_to(pull, (K, 128))], axis=1)
        g = c * x + dot(d_bf, x.astype(BF))
        h = dot(y_bf, g.astype(BF))
        g = 1.5 * g - 0.5 * (c * h + dot(d_bf, h.astype(BF)))
        shift = jnp.sum(g[:, 0:128] * g[:, 128:256], axis=0, keepdims=True) * scale
        final = centers[t] + shift + jnp.sqrt(float(K - 1) * scale) * g[:, 0:128]
        send_back[:, t] = final.astype(BF).reshape(NMEM, MEM_DEV, 128)

    back_copies = [exchange(d, send_back, back, back_send, back_recv) for d in range(1, NMEM)]
    for copy in back_copies:
        copy.start()
    back[m] = send_back[m]
    for copy in back_copies:
        copy.wait_recv()

    order = cell_order(True)
    for p in range(2):
        for half in range(2):
            tiles = [
                back[4 * half + q // 2, 2 * p + q % 2].astype(F32) for q in range(8)
            ]
            for c, channel in enumerate(block_swap(tiles)):
                rel_b[half, pl.ds(c, MEM_DEV, stride=C), :] = channel
        cells = jnp.concatenate([rel_b[0], rel_b[1]], axis=1).astype(BF)
        out_ref[:, 256 * p : 256 * p + 256] = dot(cells, order).astype(BF)

    @pl.when(r < NREG - 1)
    def _():
        halo_copy(True).wait_send()

    @pl.when(r > 0)
    def _():
        halo_copy(False).wait_send()

    for copy in tile_copies:
        copy.wait_send()
    for slot, (dr, dm) in enumerate(NEAR):
        if slot == 4:
            continue

        @pl.when(inside(dr, dm))
        def _(slot=slot):
            near_copy(slot).wait_send()

    for copy in back_copies:
        copy.wait_send()


def body(
    ensemble,
    conv_first,
    bias_first,
    conv_second,
    bias_second,
    observed_cell,
    observed_value,
    observed_precision,
):
    vmem = pl.BlockSpec(memory_space=pltpu.VMEM)
    rows = NPC * MEM_DEV
    result = pl.pallas_call(
        kernel,
        out_shape=jax.ShapeDtypeStruct((MEM_DEV * C, 512), BF),
        in_specs=[vmem] * 8,
        out_specs=vmem,
        scratch_shapes=[
            pltpu.VMEM((24, 2, 2, 128, 128), F32),
            pltpu.VMEM((2, 6, 256, 256), BF),
            pltpu.VMEM((2, 6, 256, 256), BF),
            pltpu.VMEM((2, 4, NPC + 2, MEM_DEV, 128), BF),
            pltpu.VMEM((4, rows, 256), BF),
            pltpu.VMEM((4, 4, rows, 256), BF),
            pltpu.VMEM((2, 256, 128), F32),
            pltpu.VMEM((2, 256, 128), F32),
            pltpu.VMEM((NMEM, 4, MEM_DEV, 128), BF),
            pltpu.VMEM((NMEM, 4, MEM_DEV, 128), BF),
            pltpu.VMEM((9, K + 16, 128), BF),
            pltpu.VMEM((4, K, 9 * 128), BF),
            pltpu.VMEM((4, 16, 128), F32),
            pltpu.VMEM((NMEM, 4, MEM_DEV, 128), BF),
            pltpu.VMEM((NMEM, 4, MEM_DEV, 128), BF),
            pltpu.SemaphoreType.DMA((2,)),
            pltpu.SemaphoreType.DMA((2,)),
            pltpu.SemaphoreType.DMA((NMEM,)),
            pltpu.SemaphoreType.DMA((NMEM,)),
            pltpu.SemaphoreType.DMA((9,)),
            pltpu.SemaphoreType.DMA((9,)),
            pltpu.SemaphoreType.DMA((NMEM,)),
            pltpu.SemaphoreType.DMA((NMEM,)),
        ],
        compiler_params=pltpu.CompilerParams(
            collective_id=0, has_side_effects=True, vmem_limit_bytes=48 * 1024 * 1024
        ),
    )(
        ensemble.reshape(MEM_DEV * C, 512),
        conv_first.reshape(2 * 9 * C, HID),
        bias_first,
        conv_second.reshape(2 * 9 * HID, C),
        bias_second,
        observed_cell,
        observed_value,
        observed_precision,
    )
    return result.reshape(MEM_DEV, C, 512)


def solution(mesh):
    in_specs = (
        P("mem", None, "reg"),
        P(),
        P(),
        P(),
        P(),
        P("reg", "mem", None),
        P("reg", "mem", None),
        P("reg", "mem", None),
    )
    out_specs = P("mem", None, "reg")
    return jax.shard_map(body, mesh=mesh, in_specs=in_specs, out_specs=out_specs, check_vma=False)
```

```python
import jax
import jax.numpy as jnp
from jax import lax
from jax.experimental import pallas as pl
from jax.experimental.pallas import tpu as pltpu
from jax.sharding import PartitionSpec as P

K = 256
C = 8
HID = 64
NMEM = 8
NREG = 32
MEM_DEV = 32
NPC = 16
BF = jnp.bfloat16
F32 = jnp.float32
NEAR = [(dr, dm) for dr in (-1, 0, 1) for dm in (-1, 0, 1)]
TOP, BOTTOM = 4, 5


def dot(a, b):
    return lax.dot_general(a, b, (((1,), (0,)), ((), ())), preferred_element_type=F32)


def dot_nt(a, b):
    return lax.dot_general(a, b, (((1,), (1,)), ((), ())), preferred_element_type=F32)


def iota(shape, dim):
    return lax.broadcasted_iota(jnp.int32, shape, dim)


def block_swap(arrays):
    block = iota(arrays[0].shape, 1) // 16
    for step in (1, 2, 4):
        high = (block & step) != 0
        swapped = list(arrays)
        for a in range(8):
            if a & step:
                continue
            b = a | step
            swapped[a] = jnp.where(high, pltpu.roll(arrays[b], 16 * step, 1), arrays[a])
            swapped[b] = jnp.where(high, arrays[b], pltpu.roll(arrays[a], 128 - 16 * step, 1))
        arrays = swapped
    return arrays


def cell_order(inverse):
    plain, tiled = iota((256, 256), 1 if inverse else 0), iota((256, 256), 0 if inverse else 1)
    source = ((tiled // 4) % 4) * 64 + (tiled // 16) * 4 + tiled % 4
    return jnp.where(plain == source, 1.0, 0.0).astype(BF)


def strips_of(taps, flip):
    zero = jnp.zeros((C, HID), F32)
    strips = {}
    for row_step in (-1, 0, 1):
        for col in range(-1, 5):
            pieces = []
            for j in range(4):
                step = j - col if flip else col - j
                pieces.append(taps[3 * (row_step + 1) + step + 1] if abs(step) <= 1 else zero)
            strips[row_step, col] = jnp.concatenate(pieces, axis=1)
    return strips


def build_weights(taps, flip, raw, base):
    strips = strips_of(taps, flip)
    for tile in range(6):
        for row in range(4):
            if flip:
                hidden_row = {TOP: -1, BOTTOM: 4}.get(tile, tile)
                step = hidden_row - row
            else:
                step = {TOP: row - 4, BOTTOM: row + 4 - 3}.get(tile, row - tile)
            if abs(step) > 1:
                continue
            for side in (0, 1):
                for j in range(4):
                    col = j
                    if side:
                        col = {0: 4, 3: -1}.get(j)
                    if col is None:
                        continue
                    rows = pl.ds(4 * row + j, C, stride=16)
                    raw[base + tile, side, 0, rows, :] = strips[step, col][:, 0:128]
                    raw[base + tile, side, 1, rows, :] = strips[step, col][:, 128:256]


def kernel(
    ens_ref,
    first_ref,
    bias_a_ref,
    second_ref,
    bias_b_ref,
    cell_ref,
    value_ref,
    prec_ref,
    out_ref,
    rows_of,
    picker,
    seen_send,
    seen_all,
    seen_side,
    raw,
    w_a,
    w_b,
    field,
    wide,
    hid,
    rel,
    rel_b,
    send_tiles,
    members,
    near,
    local,
    decay,
    send_back,
    back,
    halo_send,
    halo_recv,
    tile_send,
    tile_recv,
    near_send,
    near_recv,
    back_send,
    back_recv,
    rows_send,
    rows_recv,
    seen_send_sem,
    seen_recv_sem,
    side_send,
    side_recv,
):
    m = lax.axis_index("mem")
    r = lax.axis_index("reg")
    barrier = pltpu.get_barrier_semaphore()

    def inside(dr, dm):
        return (r + dr >= 0) & (r + dr < NREG) & (m + dm >= 0) & (m + dm < NMEM)

    def peer(d):
        return lax.rem(m + d, NMEM)

    def middle(index):
        return (index == NMEM // 2 - 1) | (index == NMEM // 2)

    def crosses(dm):
        if dm == 0:
            return jnp.bool_(False)
        return m == (NMEM // 2 - 1 if dm > 0 else NMEM // 2)

    for d in range(1, NMEM):
        pl.semaphore_signal(
            barrier, inc=1, device_id={"mem": peer(d), "reg": r}, device_id_type=pl.DeviceIdType.MESH
        )
    arrivals = jnp.int32(NMEM - 1)
    for dr, dm in NEAR:
        if dr == 0:
            continue

        @pl.when(inside(dr, dm))
        def _(dr=dr, dm=dm):
            pl.semaphore_signal(
                barrier,
                inc=1,
                device_id={"mem": m + dm, "reg": r + dr},
                device_id_type=pl.DeviceIdType.MESH,
            )

        arrivals = arrivals + jnp.where(inside(dr, dm), 1, 0)

    order = cell_order(False)
    for p in range(2):
        cells = dot(ens_ref[:, 256 * p : 256 * p + 256], order)
        rel[0] = cells[:, 0:128]
        rel[1] = cells[:, 128:256]
        for half in range(2):
            channels = [rel[half, pl.ds(c, MEM_DEV, stride=C), :] for c in range(C)]
            for q, tile in enumerate(block_swap(channels)):
                field[0, 1 + p, 1 + 8 * half + q] = tile.astype(BF)
    edge = jnp.zeros((MEM_DEV, 128), BF)
    for f in range(2):
        for p in range(4):
            field[f, p, 0] = edge
            field[f, p, NPC + 1] = edge

    @pl.when(r == 0)
    def _():
        field[0, 0, 1 : NPC + 1] = jnp.zeros((NPC, MEM_DEV, 128), BF)

    @pl.when(r == NREG - 1)
    def _():
        field[0, 3, 1 : NPC + 1] = jnp.zeros((NPC, MEM_DEV, 128), BF)

    for slot, (dr, dm) in enumerate(NEAR):
        if (dr, dm) == (0, 0):
            continue

        @pl.when(jnp.logical_not(inside(dr, dm)))
        def _(slot=slot):
            near[slot] = jnp.zeros((K + 16, 128), BF)

    def row_of(ref):
        return jnp.concatenate([ref[t // 2, t % 2 : t % 2 + 1, :] for t in range(4)], axis=1)

    rows_of[m] = jnp.concatenate(
        [row_of(cell_ref).astype(F32), row_of(value_ref), row_of(prec_ref), jnp.zeros((5, 128), F32)],
        axis=0,
    )

    pl.semaphore_wait(barrier, arrivals)

    def exchange(d, source, target, send_sem, recv_sem, own=None):
        return pltpu.make_async_remote_copy(
            src_ref=source.at[peer(d) if own is None else own],
            dst_ref=target.at[m],
            send_sem=send_sem.at[d],
            recv_sem=recv_sem.at[d],
            device_id={"mem": peer(d), "reg": r},
            device_id_type=pl.DeviceIdType.MESH,
        )

    def halo_copy(down):
        return pltpu.make_async_remote_copy(
            src_ref=field.at[0, 2 if down else 1, pl.ds(1, NPC)],
            dst_ref=field.at[0, 0 if down else 3, pl.ds(1, NPC)],
            send_sem=halo_send.at[1 if down else 0],
            recv_sem=halo_recv.at[1 if down else 0],
            device_id={"mem": m, "reg": r + 1 if down else r - 1},
            device_id_type=pl.DeviceIdType.MESH,
        )

    @pl.when(r < NREG - 1)
    def _():
        halo_copy(True).start()

    @pl.when(r > 0)
    def _():
        halo_copy(False).start()

    rows_copies = [exchange(d, rows_of, rows_of, rows_send, rows_recv, m) for d in range(1, NMEM)]
    for copy in rows_copies:
        copy.start()

    raw[...] = jnp.zeros(raw.shape, F32)
    for f in range(2):
        taps = [
            0.5 * first_ref[pl.ds((9 * f + t) * C, C), :].astype(F32) for t in range(9)
        ]
        build_weights(taps, False, raw, 12 * f)
        taps = [second_ref[pl.ds((9 * f + t) * C, C), :].astype(F32) for t in range(9)]
        build_weights(taps, True, raw, 12 * f + 6)
        for tile in range(6):
            for side in range(2):
                span = slice(128 * side, 128 * side + 128)
                for part in range(2):
                    lanes = slice(128 * part, 128 * part + 128)
                    w_a[f, tile, span, lanes] = raw[12 * f + tile, side, part].astype(BF)
                    w_b[f, tile, lanes, span] = jnp.transpose(
                        raw[12 * f + 6 + tile, side, part]
                    ).astype(BF)

    lane = iota((1, 128), 1)
    for target in range(4):
        for slot, (dr, dm) in enumerate(NEAR):
            a = 2 * dr + lane // 64 - target // 2
            b = 2 * dm + (lane // 32) % 2 - target % 2
            keep = (jnp.abs(a) <= 2) & (jnp.abs(b) <= 2) & inside(dr, dm)
            fall = jnp.exp((a * a + b * b).astype(F32) * (-1.0 / 9.0))
            decay[target, slot : slot + 1, :] = jnp.where(keep, fall, 0.0)

    row_lane = iota((1, 1, 128), 2)
    bias_lane = iota((1, 128), 1)
    keep_top = jnp.where(r == 0, 0.0, 1.0).astype(F32)
    keep_bottom = jnp.where(r == NREG - 1, 0.0, 1.0).astype(F32)
    keep = (keep_top, None, None, keep_bottom)

    def widen(f, p):
        right = field[f, p, 2 : NPC + 2].astype(F32)
        left = field[f, p, 0:NPC].astype(F32)
        side = jnp.where(row_lane % 4 < 2, right, left).astype(BF)
        wide[p, :, 0:128] = field[f, p, 1 : NPC + 1].reshape(NPC * MEM_DEV, 128)
        wide[p, :, 128:256] = side.reshape(NPC * MEM_DEV, 128)

    def hidden(f, p, i, bias):
        total = dot(wide[p], w_a[f, i])
        if i == 0:
            total = total + dot(wide[p - 1], w_a[f, TOP])
        if i == 3:
            total = total + dot(wide[p + 1], w_a[f, BOTTOM])
        total = total + bias
        total = total + total * jnp.tanh(total)
        if keep[p] is not None:
            total = total * keep[p]
        hid[p, i] = total.astype(BF)

    def branch(f, p, bias):
        total = None
        terms = [(p, i, i) for i in range(4)] + [(p - 1, 3, TOP), (p + 1, 0, BOTTOM)]
        if p == 0:
            terms = [(0, 1, 1), (0, 2, 2), (0, 3, 3), (1, 0, BOTTOM)]
        if p == 3:
            terms = [(3, 0, 0), (3, 1, 1), (3, 2, 2), (2, 3, TOP)]
        for hp, hi, tile in terms:
            part = dot(hid[hp, hi], w_b[f, tile])
            total = part if total is None else total + part
        own = total[:, 0:128].reshape(NPC, MEM_DEV, 128)
        side = total[:, 128:256].reshape(NPC, MEM_DEV, 128)
        none = jnp.zeros((1, MEM_DEV, 128), F32)
        before = jnp.concatenate([none, side[: NPC - 1]], axis=0)
        after = jnp.concatenate([side[1:], none], axis=0)
        moved = jnp.where(row_lane % 4 < 2, before, after)
        result = field[f, p, 1 : NPC + 1].astype(F32) + (own + moved + bias[None])
        if keep[p] is not None:
            result = result * keep[p]
        return result.astype(BF)

    def biases(f):
        half = 0.5 * bias_a_ref[f : f + 1, :]
        first = jnp.concatenate([half] * 4, axis=1)
        second = jnp.zeros((1, 128), F32)
        for c in range(C):
            second = jnp.where(bias_lane // 16 == c, bias_b_ref[f : f + 1, c : c + 1], second)
        return first, second

    bias_a, bias_b = biases(0)
    widen(0, 1)
    widen(0, 2)
    for p, i in ((1, 1), (1, 2), (2, 1), (2, 2), (1, 3), (2, 0)):
        hidden(0, p, i, bias_a)

    @pl.when(r < NREG - 1)
    def _():
        halo_copy(False).wait_recv()

    @pl.when(r > 0)
    def _():
        halo_copy(True).wait_recv()

    widen(0, 0)
    widen(0, 3)
    for p, i in ((1, 0), (2, 3), (0, 1), (0, 2), (0, 3), (3, 0), (3, 1), (3, 2)):
        hidden(0, p, i, bias_a)
    for p in range(4):
        field[1, p, 1 : NPC + 1] = branch(0, p, bias_b)

    for copy in rows_copies:
        copy.wait_recv()
    for b in range(NMEM):
        cells = rows_of[b, 0:1, :]
        picker[b] = jnp.where(iota((128, 128), 0).astype(F32) == cells, 1.0, 0.0).astype(BF)

    bias_a, bias_b = biases(1)
    for p in range(4):
        widen(1, p)
    hidden(1, 0, 3, bias_a)
    hidden(1, 3, 0, bias_a)
    for p in (1, 2):
        for i in range(4):
            hidden(1, p, i, bias_a)
    for p in (1, 2):
        tiles = branch(1, p, bias_b).reshape(NMEM, 2, MEM_DEV, 128)
        for ql in range(2):
            send_tiles[:, 2 * (p - 1) + ql] = tiles[:, ql]

    for b in range(NMEM):
        found = dot(send_tiles[b].reshape(4 * MEM_DEV, 128), picker[b])
        seen = found[0:MEM_DEV]
        for t in range(1, 4):
            seen = jnp.where(lane // 32 == t, found[MEM_DEV * t : MEM_DEV * t + MEM_DEV], seen)
        seen_send[b] = seen.astype(BF)

    def side_copy(d):
        return pltpu.make_async_remote_copy(
            src_ref=seen_send.at[NMEM - 1 - peer(d)],
            dst_ref=seen_side.at[m],
            send_sem=side_send.at[d],
            recv_sem=side_recv.at[d],
            device_id={"mem": peer(d), "reg": r},
            device_id_type=pl.DeviceIdType.MESH,
        )

    seen_copies = [
        exchange(d, seen_send, seen_all, seen_send_sem, seen_recv_sem) for d in range(1, NMEM)
    ]
    for copy in seen_copies:
        copy.start()
    for d in range(1, NMEM):

        @pl.when(middle(peer(d)))
        def _(d=d):
            side_copy(d).start()

    seen_all[m] = seen_send[m]
    for copy in seen_copies:
        copy.wait_recv()

    def anomalies(values, owner, slot):
        seen = values[...].reshape(K, 128).astype(F32)
        center = jnp.sum(seen, axis=0, keepdims=True) * (1.0 / K)
        root = jnp.sqrt(rows_of[owner, 2:3, :])
        near[slot, 0:K] = ((seen - center) * root).astype(BF)
        depart = (rows_of[owner, 1:2, :] - center) * root
        high = depart.astype(BF).astype(F32)
        sub = iota((16, 128), 0)
        near[slot, K : K + 16] = jnp.where(
            sub == 0, high, jnp.where(sub == 1, depart - high, 0.0)
        ).astype(BF)

    anomalies(seen_all, m, 4)

    def near_copy(slot):
        dr, dm = NEAR[slot]
        return pltpu.make_async_remote_copy(
            src_ref=near.at[4],
            dst_ref=near.at[8 - slot],
            send_sem=near_send.at[slot],
            recv_sem=near_recv.at[8 - slot],
            device_id={"mem": m + dm, "reg": r + dr},
            device_id_type=pl.DeviceIdType.MESH,
        )

    for slot, (dr, dm) in enumerate(NEAR):
        if slot == 4:
            continue

        @pl.when(inside(dr, dm) & jnp.logical_not(crosses(dm)))
        def _(slot=slot):
            near_copy(slot).start()

    def cross_copy(dr, dm):
        return pltpu.make_async_remote_copy(
            src_ref=near.at[4 + dm],
            dst_ref=near.at[3 * (1 - dr) + 1 + dm],
            send_sem=near_send.at[3 * (1 + dr) + 1 + dm],
            recv_sem=near_recv.at[3 * (1 - dr) + 1 + dm],
            device_id={"mem": m, "reg": r + dr},
            device_id_type=pl.DeviceIdType.MESH,
        )

    for dm in (-1, 1):

        @pl.when(crosses(dm))
        def _(dm=dm):
            seen_side[m] = seen_send[NMEM - 1 - m]
            for d in range(1, NMEM):
                side_copy(d).wait_recv()
            anomalies(seen_side, NMEM - 1 - m, 4 + dm)

        for dr in (-1, 1):

            @pl.when(crosses(dm) & inside(dr, dm))
            def _(dr=dr, dm=dm):
                cross_copy(dr, dm).start()

    tile_copies = [exchange(d, send_tiles, members, tile_send, tile_recv) for d in range(1, NMEM)]
    for copy in tile_copies:
        copy.start()
    members[m] = send_tiles[m]

    for slot, (dr, dm) in enumerate(NEAR):
        if slot == 4:
            continue

        arrives = inside(dr, dm)
        if dr == 0:
            arrives = arrives & jnp.logical_not(crosses(dm))

        @pl.when(arrives)
        def _(slot=slot):
            near_copy(8 - slot).wait_recv()

    summed = jnp.zeros((K, 8), F32)
    for slot in range(9):
        block = near[slot, 0:K].astype(F32)
        tail = near[slot, K : K + 16].astype(F32)
        depart = tail[0:1] + tail[1:2]
        pulls = []
        for t in range(4):
            fall = decay[t, slot : slot + 1, :]
            local[t, :, 128 * slot : 128 * slot + 128] = (block * fall).astype(BF)
            pulls.append(fall * fall * depart)
        pulls = jnp.concatenate(pulls, axis=0)
        high = pulls.astype(BF).astype(F32)
        both = jnp.concatenate([high, pulls - high], axis=0).astype(BF)
        summed = summed + dot_nt(near[slot, 0:K], both)

    eye = jnp.where(iota((K, K), 0) == iota((K, K), 1), float(K - 1), 0.0)

    def solve(patches):
        scale, ys, ds = [], [], []
        for t in patches:
            system = dot_nt(local[t], local[t]) + eye
            rows = jnp.sum(jnp.abs(system), axis=0, keepdims=True)
            scale.append(1.0 / jnp.max(rows, axis=1, keepdims=True))
            ds.append(system * scale[-1])
        lows = [a.astype(BF) for a in ds]
        ys = [1.5 * a - 0.5 * dot(low, low) for a, low in zip(ds, lows)]
        ds = [-0.5 * a for a in ds]
        c = 1.5
        for _ in range(2):
            y_low = [y.astype(BF) for y in ys]
            d_low = [d.astype(BF) for d in ds]
            ms = [c * y + dot(dl, yl) for y, dl, yl in zip(ys, d_low, y_low)]
            m_low = [mm.astype(BF) for mm in ms]
            ys = [1.5 * y - 0.5 * dot(yl, ml) for y, yl, ml in zip(ys, y_low, m_low)]
            ds = [
                1.5 * d - (0.5 * c) * mm - 0.5 * dot(ml, dl)
                for d, mm, ml, dl in zip(ds, ms, m_low, d_low)
            ]
            c = 1.5 * c
        y_low = [y.astype(BF) for y in ys]
        d_low = [d.astype(BF) for d in ds]
        xs = []
        if patches[0] == 0:
            for copy in tile_copies:
                copy.wait_recv()
        centers = {}
        for t in patches:
            tile = members[:, t].reshape(K, 128).astype(F32)
            centers[t] = jnp.sum(tile, axis=0, keepdims=True) * (1.0 / K)
            spread = tile - centers[t]
            pull = summed[:, t : t + 1] + summed[:, 4 + t : 5 + t]
            xs.append(jnp.concatenate([spread, jnp.broadcast_to(pull, (K, 128))], axis=1))
        gs = [c * x + dot(dl, x.astype(BF)) for x, dl in zip(xs, d_low)]
        hs = [dot(yl, g.astype(BF)) for yl, g in zip(y_low, gs)]
        gs = [
            1.5 * g - 0.5 * (c * h + dot(dl, h.astype(BF))) for g, h, dl in zip(gs, hs, d_low)
        ]
        for t, g, sc in zip(patches, gs, scale):
            shift = jnp.sum(g[:, 0:128] * g[:, 128:256], axis=0, keepdims=True) * sc
            final = centers[t] + shift + jnp.sqrt(float(K - 1) * sc) * g[:, 0:128]
            send_back[t // 2, :, t % 2] = final.astype(BF).reshape(NMEM, MEM_DEV, 128)

    back_copies = []
    for half in range(2):
        solve((2 * half, 2 * half + 1))
        copies = [
            exchange(d, send_back.at[half], back.at[half], back_send.at[half], back_recv.at[half])
            for d in range(1, NMEM)
        ]
        for copy in copies:
            copy.start()
        back[half, m] = send_back[half, m]
        back_copies.append(copies)

    order = cell_order(True)
    for p in range(2):
        for copy in back_copies[p]:
            copy.wait_recv()
        for half in range(2):
            tiles = [back[p, 4 * half + q // 2, q % 2].astype(F32) for q in range(8)]
            for c, channel in enumerate(block_swap(tiles)):
                rel_b[half, pl.ds(c, MEM_DEV, stride=C), :] = channel
        cells = jnp.concatenate([rel_b[0], rel_b[1]], axis=1).astype(BF)
        out_ref[:, 256 * p : 256 * p + 256] = dot(cells, order).astype(BF)

    @pl.when(r < NREG - 1)
    def _():
        halo_copy(True).wait_send()

    @pl.when(r > 0)
    def _():
        halo_copy(False).wait_send()

    for copy in rows_copies + seen_copies + tile_copies:
        copy.wait_send()
    for d in range(1, NMEM):

        @pl.when(middle(peer(d)))
        def _(d=d):
            side_copy(d).wait_send()

    for slot, (dr, dm) in enumerate(NEAR):
        if slot == 4:
            continue

        leaves = inside(dr, dm)
        if dr == 0:
            leaves = leaves & jnp.logical_not(crosses(dm))

        @pl.when(leaves)
        def _(slot=slot):
            near_copy(slot).wait_send()

    for copies in back_copies:
        for copy in copies:
            copy.wait_send()


def body(
    ensemble,
    conv_first,
    bias_first,
    conv_second,
    bias_second,
    observed_cell,
    observed_value,
    observed_precision,
):
    vmem = pl.BlockSpec(memory_space=pltpu.VMEM)
    rows = NPC * MEM_DEV
    result = pl.pallas_call(
        kernel,
        out_shape=jax.ShapeDtypeStruct((MEM_DEV * C, 512), BF),
        in_specs=[vmem] * 8,
        out_specs=vmem,
        scratch_shapes=[
            pltpu.VMEM((NMEM, 8, 128), F32),
            pltpu.VMEM((NMEM, 128, 128), BF),
            pltpu.VMEM((NMEM, MEM_DEV, 128), BF),
            pltpu.VMEM((NMEM, MEM_DEV, 128), BF),
            pltpu.VMEM((NMEM, MEM_DEV, 128), BF),
            pltpu.VMEM((24, 2, 2, 128, 128), F32),
            pltpu.VMEM((2, 6, 256, 256), BF),
            pltpu.VMEM((2, 6, 256, 256), BF),
            pltpu.VMEM((2, 4, NPC + 2, MEM_DEV, 128), BF),
            pltpu.VMEM((4, rows, 256), BF),
            pltpu.VMEM((4, 4, rows, 256), BF),
            pltpu.VMEM((2, 256, 128), F32),
            pltpu.VMEM((2, 256, 128), F32),
            pltpu.VMEM((NMEM, 4, MEM_DEV, 128), BF),
            pltpu.VMEM((NMEM, 4, MEM_DEV, 128), BF),
            pltpu.VMEM((9, K + 16, 128), BF),
            pltpu.VMEM((4, K, 9 * 128), BF),
            pltpu.VMEM((4, 16, 128), F32),
            pltpu.VMEM((2, NMEM, 2, MEM_DEV, 128), BF),
            pltpu.VMEM((2, NMEM, 2, MEM_DEV, 128), BF),
            pltpu.SemaphoreType.DMA((2,)),
            pltpu.SemaphoreType.DMA((2,)),
            pltpu.SemaphoreType.DMA((NMEM,)),
            pltpu.SemaphoreType.DMA((NMEM,)),
            pltpu.SemaphoreType.DMA((9,)),
            pltpu.SemaphoreType.DMA((9,)),
            pltpu.SemaphoreType.DMA((2, NMEM)),
            pltpu.SemaphoreType.DMA((2, NMEM)),
            pltpu.SemaphoreType.DMA((NMEM,)),
            pltpu.SemaphoreType.DMA((NMEM,)),
            pltpu.SemaphoreType.DMA((NMEM,)),
            pltpu.SemaphoreType.DMA((NMEM,)),
            pltpu.SemaphoreType.DMA((NMEM,)),
            pltpu.SemaphoreType.DMA((NMEM,)),
        ],
        compiler_params=pltpu.CompilerParams(
            collective_id=0, has_side_effects=True, vmem_limit_bytes=48 * 1024 * 1024
        ),
    )(
        ensemble.reshape(MEM_DEV * C, 512),
        conv_first.reshape(2 * 9 * C, HID),
        bias_first,
        conv_second.transpose(0, 1, 3, 2).reshape(2 * 9 * C, HID),
        bias_second,
        observed_cell,
        observed_value,
        observed_precision,
    )
    return result.reshape(MEM_DEV, C, 512)


def solution(mesh):
    in_specs = (
        P("mem", None, "reg"),
        P(),
        P(),
        P(),
        P(),
        P("reg", "mem", None),
        P("reg", "mem", None),
        P("reg", "mem", None),
    )
    out_specs = P("mem", None, "reg")
    return jax.shard_map(body, mesh=mesh, in_specs=in_specs, out_specs=out_specs, check_vma=False)
```

```python
import jax
import jax.numpy as jnp
from jax import lax
from jax.experimental import pallas as pl
from jax.experimental.pallas import tpu as pltpu
from jax.sharding import PartitionSpec as P

K = 256
C = 8
HID = 64
NMEM = 8
NREG = 32
MEM_DEV = 32
NPC = 16
BF = jnp.bfloat16
F32 = jnp.float32
NEAR = [(dr, dm) for dr in (-1, 0, 1) for dm in (-1, 0, 1)]
TOP, BOTTOM = 4, 5


def dot(a, b):
    return lax.dot_general(a, b, (((1,), (0,)), ((), ())), preferred_element_type=F32)


def dot_nt(a, b):
    return lax.dot_general(a, b, (((1,), (1,)), ((), ())), preferred_element_type=F32)


def iota(shape, dim):
    return lax.broadcasted_iota(jnp.int32, shape, dim)


def block_swap(arrays):
    block = iota(arrays[0].shape, 1) // 16
    for step in (1, 2, 4):
        high = (block & step) != 0
        swapped = list(arrays)
        for a in range(8):
            if a & step:
                continue
            b = a | step
            swapped[a] = jnp.where(high, pltpu.roll(arrays[b], 16 * step, 1), arrays[a])
            swapped[b] = jnp.where(high, arrays[b], pltpu.roll(arrays[a], 128 - 16 * step, 1))
        arrays = swapped
    return arrays


def cell_order(inverse):
    plain, tiled = iota((256, 256), 1 if inverse else 0), iota((256, 256), 0 if inverse else 1)
    source = ((tiled // 4) % 4) * 64 + (tiled // 16) * 4 + tiled % 4
    return jnp.where(plain == source, 1.0, 0.0).astype(BF)


def strips_of(taps, flip):
    zero = jnp.zeros((C, HID), F32)
    strips = {}
    for row_step in (-1, 0, 1):
        for col in range(-1, 5):
            pieces = []
            for j in range(4):
                step = j - col if flip else col - j
                pieces.append(taps[3 * (row_step + 1) + step + 1] if abs(step) <= 1 else zero)
            strips[row_step, col] = jnp.concatenate(pieces, axis=1)
    return strips


def build_weights(taps, flip, raw, base):
    strips = strips_of(taps, flip)
    for tile in range(6):
        for row in range(4):
            if flip:
                hidden_row = {TOP: -1, BOTTOM: 4}.get(tile, tile)
                step = hidden_row - row
            else:
                step = {TOP: row - 4, BOTTOM: row + 4 - 3}.get(tile, row - tile)
            if abs(step) > 1:
                continue
            for side in (0, 1):
                for j in range(4):
                    col = j
                    if side:
                        col = {0: 4, 3: -1}.get(j)
                    if col is None:
                        continue
                    rows = pl.ds(4 * row + j, C, stride=16)
                    raw[base + tile, side, 0, rows, :] = strips[step, col][:, 0:128]
                    raw[base + tile, side, 1, rows, :] = strips[step, col][:, 128:256]


def kernel(
    ens_hbm,
    first_hbm,
    bias_a_hbm,
    second_hbm,
    bias_b_hbm,
    cell_hbm,
    value_hbm,
    prec_hbm,
    out_ref,
    ens_ref,
    first_ref,
    bias_a_ref,
    second_ref,
    bias_b_ref,
    cell_ref,
    value_ref,
    prec_ref,
    load_sem,
    rows_of,
    picker,
    seen_send,
    seen_all,
    seen_side,
    raw,
    w_a,
    w_b,
    field,
    wide,
    hid,
    rel,
    rel_b,
    send_tiles,
    members,
    near,
    local,
    decay,
    send_back,
    back,
    halo_send,
    halo_recv,
    tile_send,
    tile_recv,
    near_send,
    near_recv,
    back_send,
    back_recv,
    rows_send,
    rows_recv,
    seen_send_sem,
    seen_recv_sem,
    side_send,
    side_recv,
):
    m = lax.axis_index("mem")
    r = lax.axis_index("reg")
    barrier = pltpu.get_barrier_semaphore()

    def inside(dr, dm):
        return (r + dr >= 0) & (r + dr < NREG) & (m + dm >= 0) & (m + dm < NMEM)

    def peer(d):
        return lax.rem(m + d, NMEM)

    def middle(index):
        return (index == NMEM // 2 - 1) | (index == NMEM // 2)

    def crosses(dm):
        if dm == 0:
            return jnp.bool_(False)
        return m == (NMEM // 2 - 1 if dm > 0 else NMEM // 2)

    for d in range(1, NMEM):
        pl.semaphore_signal(
            barrier, inc=1, device_id={"mem": peer(d), "reg": r}, device_id_type=pl.DeviceIdType.MESH
        )
    arrivals = jnp.int32(NMEM - 1)
    for dr, dm in NEAR:
        if dr == 0:
            continue

        @pl.when(inside(dr, dm))
        def _(dr=dr, dm=dm):
            pl.semaphore_signal(
                barrier,
                inc=1,
                device_id={"mem": m + dm, "reg": r + dr},
                device_id_type=pl.DeviceIdType.MESH,
            )

        arrivals = arrivals + jnp.where(inside(dr, dm), 1, 0)

    loads = [
        pltpu.make_async_copy(source, target, load_sem.at[i])
        for i, (source, target) in enumerate(
            (
                (ens_hbm, ens_ref),
                (first_hbm, first_ref),
                (bias_a_hbm, bias_a_ref),
                (second_hbm, second_ref),
                (bias_b_hbm, bias_b_ref),
                (cell_hbm, cell_ref),
                (value_hbm, value_ref),
                (prec_hbm, prec_ref),
            )
        )
    ]
    for load in loads:
        load.start()

    order = cell_order(False)
    loads[0].wait()
    for p in range(2):
        cells = dot(ens_ref[:, 256 * p : 256 * p + 256], order)
        rel[0] = cells[:, 0:128]
        rel[1] = cells[:, 128:256]
        for half in range(2):
            channels = [rel[half, pl.ds(c, MEM_DEV, stride=C), :] for c in range(C)]
            for q, tile in enumerate(block_swap(channels)):
                field[0, 1 + p, 1 + 8 * half + q] = tile.astype(BF)
    edge = jnp.zeros((MEM_DEV, 128), BF)
    for f in range(2):
        for p in range(4):
            field[f, p, 0] = edge
            field[f, p, NPC + 1] = edge

    @pl.when(r == 0)
    def _():
        field[0, 0, 1 : NPC + 1] = jnp.zeros((NPC, MEM_DEV, 128), BF)

    @pl.when(r == NREG - 1)
    def _():
        field[0, 3, 1 : NPC + 1] = jnp.zeros((NPC, MEM_DEV, 128), BF)

    for slot, (dr, dm) in enumerate(NEAR):
        if (dr, dm) == (0, 0):
            continue

        @pl.when(jnp.logical_not(inside(dr, dm)))
        def _(slot=slot):
            near[slot] = jnp.zeros((K + 16, 128), BF)

    for load in loads[1:]:
        load.wait()

    def row_of(ref):
        return jnp.concatenate([ref[t // 2, t % 2 : t % 2 + 1, :] for t in range(4)], axis=1)

    rows_of[m] = jnp.concatenate(
        [row_of(cell_ref).astype(F32), row_of(value_ref), row_of(prec_ref), jnp.zeros((5, 128), F32)],
        axis=0,
    )

    pl.semaphore_wait(barrier, arrivals)

    def exchange(d, source, target, send_sem, recv_sem, own=None):
        return pltpu.make_async_remote_copy(
            src_ref=source.at[peer(d) if own is None else own],
            dst_ref=target.at[m],
            send_sem=send_sem.at[d],
            recv_sem=recv_sem.at[d],
            device_id={"mem": peer(d), "reg": r},
            device_id_type=pl.DeviceIdType.MESH,
        )

    def halo_copy(down):
        return pltpu.make_async_remote_copy(
            src_ref=field.at[0, 2 if down else 1, pl.ds(1, NPC)],
            dst_ref=field.at[0, 0 if down else 3, pl.ds(1, NPC)],
            send_sem=halo_send.at[1 if down else 0],
            recv_sem=halo_recv.at[1 if down else 0],
            device_id={"mem": m, "reg": r + 1 if down else r - 1},
            device_id_type=pl.DeviceIdType.MESH,
        )

    @pl.when(r < NREG - 1)
    def _():
        halo_copy(True).start()

    @pl.when(r > 0)
    def _():
        halo_copy(False).start()

    rows_copies = [exchange(d, rows_of, rows_of, rows_send, rows_recv, m) for d in range(1, NMEM)]
    for copy in rows_copies:
        copy.start()

    raw[...] = jnp.zeros(raw.shape, F32)
    for f in range(2):
        taps = [
            0.5 * first_ref[pl.ds((9 * f + t) * C, C), :].astype(F32) for t in range(9)
        ]
        build_weights(taps, False, raw, 12 * f)
        taps = [second_ref[pl.ds((9 * f + t) * C, C), :].astype(F32) for t in range(9)]
        build_weights(taps, True, raw, 12 * f + 6)
        for tile in range(6):
            for side in range(2):
                span = slice(128 * side, 128 * side + 128)
                for part in range(2):
                    lanes = slice(128 * part, 128 * part + 128)
                    w_a[f, tile, span, lanes] = raw[12 * f + tile, side, part].astype(BF)
                    w_b[f, tile, lanes, span] = jnp.transpose(
                        raw[12 * f + 6 + tile, side, part]
                    ).astype(BF)

    lane = iota((1, 128), 1)
    for target in range(4):
        for slot, (dr, dm) in enumerate(NEAR):
            a = 2 * dr + lane // 64 - target // 2
            b = 2 * dm + (lane // 32) % 2 - target % 2
            keep = (jnp.abs(a) <= 2) & (jnp.abs(b) <= 2) & inside(dr, dm)
            fall = jnp.exp((a * a + b * b).astype(F32) * (-1.0 / 9.0))
            decay[target, slot : slot + 1, :] = jnp.where(keep, fall, 0.0)

    row_lane = iota((1, 1, 128), 2)
    bias_lane = iota((1, 128), 1)
    keep_top = jnp.where(r == 0, 0.0, 1.0).astype(F32)
    keep_bottom = jnp.where(r == NREG - 1, 0.0, 1.0).astype(F32)
    keep = (keep_top, None, None, keep_bottom)

    def widen(f, p):
        right = field[f, p, 2 : NPC + 2].astype(F32)
        left = field[f, p, 0:NPC].astype(F32)
        side = jnp.where(row_lane % 4 < 2, right, left).astype(BF)
        wide[p, :, 0:128] = field[f, p, 1 : NPC + 1].reshape(NPC * MEM_DEV, 128)
        wide[p, :, 128:256] = side.reshape(NPC * MEM_DEV, 128)

    def hidden(f, p, i, bias):
        total = dot(wide[p], w_a[f, i])
        if i == 0:
            total = total + dot(wide[p - 1], w_a[f, TOP])
        if i == 3:
            total = total + dot(wide[p + 1], w_a[f, BOTTOM])
        total = total + bias
        total = total + total * jnp.tanh(total)
        if keep[p] is not None:
            total = total * keep[p]
        hid[p, i] = total.astype(BF)

    def branch(f, p, bias):
        total = None
        terms = [(p, i, i) for i in range(4)] + [(p - 1, 3, TOP), (p + 1, 0, BOTTOM)]
        if p == 0:
            terms = [(0, 1, 1), (0, 2, 2), (0, 3, 3), (1, 0, BOTTOM)]
        if p == 3:
            terms = [(3, 0, 0), (3, 1, 1), (3, 2, 2), (2, 3, TOP)]
        for hp, hi, tile in terms:
            part = dot(hid[hp, hi], w_b[f, tile])
            total = part if total is None else total + part
        own = total[:, 0:128].reshape(NPC, MEM_DEV, 128)
        side = total[:, 128:256].reshape(NPC, MEM_DEV, 128)
        none = jnp.zeros((1, MEM_DEV, 128), F32)
        before = jnp.concatenate([none, side[: NPC - 1]], axis=0)
        after = jnp.concatenate([side[1:], none], axis=0)
        moved = jnp.where(row_lane % 4 < 2, before, after)
        result = field[f, p, 1 : NPC + 1].astype(F32) + (own + moved + bias[None])
        if keep[p] is not None:
            result = result * keep[p]
        return result.astype(BF)

    def biases(f):
        half = 0.5 * bias_a_ref[f : f + 1, :]
        first = jnp.concatenate([half] * 4, axis=1)
        second = jnp.zeros((1, 128), F32)
        for c in range(C):
            second = jnp.where(bias_lane // 16 == c, bias_b_ref[f : f + 1, c : c + 1], second)
        return first, second

    bias_a, bias_b = biases(0)
    widen(0, 1)
    widen(0, 2)
    for p, i in ((1, 1), (1, 2), (2, 1), (2, 2), (1, 3), (2, 0)):
        hidden(0, p, i, bias_a)

    @pl.when(r < NREG - 1)
    def _():
        halo_copy(False).wait_recv()

    @pl.when(r > 0)
    def _():
        halo_copy(True).wait_recv()

    widen(0, 0)
    widen(0, 3)
    for p, i in ((1, 0), (2, 3), (0, 1), (0, 2), (0, 3), (3, 0), (3, 1), (3, 2)):
        hidden(0, p, i, bias_a)
    for p in range(4):
        field[1, p, 1 : NPC + 1] = branch(0, p, bias_b)

    for copy in rows_copies:
        copy.wait_recv()
    for b in range(NMEM):
        cells = rows_of[b, 0:1, :]
        picker[b] = jnp.where(iota((128, 128), 0).astype(F32) == cells, 1.0, 0.0).astype(BF)

    bias_a, bias_b = biases(1)
    for p in range(4):
        widen(1, p)
    hidden(1, 0, 3, bias_a)
    hidden(1, 3, 0, bias_a)
    for p in (1, 2):
        for i in range(4):
            hidden(1, p, i, bias_a)
    for p in (1, 2):
        tiles = branch(1, p, bias_b).reshape(NMEM, 2, MEM_DEV, 128)
        for ql in range(2):
            send_tiles[:, 2 * (p - 1) + ql] = tiles[:, ql]

    for b in range(NMEM):
        found = dot(send_tiles[b].reshape(4 * MEM_DEV, 128), picker[b])
        seen = found[0:MEM_DEV]
        for t in range(1, 4):
            seen = jnp.where(lane // 32 == t, found[MEM_DEV * t : MEM_DEV * t + MEM_DEV], seen)
        seen_send[b] = seen.astype(BF)

    def side_copy(d):
        return pltpu.make_async_remote_copy(
            src_ref=seen_send.at[NMEM - 1 - peer(d)],
            dst_ref=seen_side.at[m],
            send_sem=side_send.at[d],
            recv_sem=side_recv.at[d],
            device_id={"mem": peer(d), "reg": r},
            device_id_type=pl.DeviceIdType.MESH,
        )

    seen_copies = [
        exchange(d, seen_send, seen_all, seen_send_sem, seen_recv_sem) for d in range(1, NMEM)
    ]
    for copy in seen_copies:
        copy.start()
    for d in range(1, NMEM):

        @pl.when(middle(peer(d)))
        def _(d=d):
            side_copy(d).start()

    tile_copies = [exchange(d, send_tiles, members, tile_send, tile_recv) for d in range(1, NMEM)]
    for copy in tile_copies:
        copy.start()
    members[m] = send_tiles[m]

    seen_all[m] = seen_send[m]
    for copy in seen_copies:
        copy.wait_recv()

    def anomalies(values, owner, slot):
        seen = values[...].reshape(K, 128).astype(F32)
        center = jnp.sum(seen, axis=0, keepdims=True) * (1.0 / K)
        root = jnp.sqrt(rows_of[owner, 2:3, :])
        near[slot, 0:K] = ((seen - center) * root).astype(BF)
        depart = (rows_of[owner, 1:2, :] - center) * root
        high = depart.astype(BF).astype(F32)
        sub = iota((16, 128), 0)
        near[slot, K : K + 16] = jnp.where(
            sub == 0, high, jnp.where(sub == 1, depart - high, 0.0)
        ).astype(BF)

    anomalies(seen_all, m, 4)

    def near_copy(slot):
        dr, dm = NEAR[slot]
        return pltpu.make_async_remote_copy(
            src_ref=near.at[4],
            dst_ref=near.at[8 - slot],
            send_sem=near_send.at[slot],
            recv_sem=near_recv.at[8 - slot],
            device_id={"mem": m + dm, "reg": r + dr},
            device_id_type=pl.DeviceIdType.MESH,
        )

    for slot, (dr, dm) in enumerate(NEAR):
        if slot == 4:
            continue

        @pl.when(inside(dr, dm) & jnp.logical_not(crosses(dm)))
        def _(slot=slot):
            near_copy(slot).start()

    def cross_copy(dr, dm):
        return pltpu.make_async_remote_copy(
            src_ref=near.at[4 + dm],
            dst_ref=near.at[3 * (1 - dr) + 1 + dm],
            send_sem=near_send.at[3 * (1 + dr) + 1 + dm],
            recv_sem=near_recv.at[3 * (1 - dr) + 1 + dm],
            device_id={"mem": m, "reg": r + dr},
            device_id_type=pl.DeviceIdType.MESH,
        )

    for dm in (-1, 1):

        @pl.when(crosses(dm))
        def _(dm=dm):
            seen_side[m] = seen_send[NMEM - 1 - m]
            for d in range(1, NMEM):
                side_copy(d).wait_recv()
            anomalies(seen_side, NMEM - 1 - m, 4 + dm)

        for dr in (-1, 1):

            @pl.when(crosses(dm) & inside(dr, dm))
            def _(dr=dr, dm=dm):
                cross_copy(dr, dm).start()

    for slot, (dr, dm) in enumerate(NEAR):
        if slot == 4:
            continue

        arrives = inside(dr, dm)
        if dr == 0:
            arrives = arrives & jnp.logical_not(crosses(dm))

        @pl.when(arrives)
        def _(slot=slot):
            near_copy(8 - slot).wait_recv()

    summed = jnp.zeros((K, 8), F32)
    for slot in range(9):
        block = near[slot, 0:K].astype(F32)
        tail = near[slot, K : K + 16].astype(F32)
        depart = tail[0:1] + tail[1:2]
        pulls = []
        for t in range(4):
            fall = decay[t, slot : slot + 1, :]
            local[t, :, 128 * slot : 128 * slot + 128] = (block * fall).astype(BF)
            pulls.append(fall * fall * depart)
        pulls = jnp.concatenate(pulls, axis=0)
        high = pulls.astype(BF).astype(F32)
        both = jnp.concatenate([high, pulls - high], axis=0).astype(BF)
        summed = summed + dot_nt(near[slot, 0:K], both)

    eye = jnp.where(iota((K, K), 0) == iota((K, K), 1), float(K - 1), 0.0)

    def solve(patches):
        scale, ys, ds = [], [], []
        for t in patches:
            system = dot_nt(local[t], local[t]) + eye
            rows = jnp.sum(jnp.abs(system), axis=0, keepdims=True)
            scale.append(1.0 / jnp.max(rows, axis=1, keepdims=True))
            ds.append(system * scale[-1])
        lows = [a.astype(BF) for a in ds]
        ys = [1.5 * a - 0.5 * dot(low, low) for a, low in zip(ds, lows)]
        ds = [-0.5 * a for a in ds]
        c = 1.5
        for _ in range(2):
            y_low = [y.astype(BF) for y in ys]
            d_low = [d.astype(BF) for d in ds]
            ms = [c * y + dot(dl, yl) for y, dl, yl in zip(ys, d_low, y_low)]
            m_low = [mm.astype(BF) for mm in ms]
            ys = [1.5 * y - 0.5 * dot(yl, ml) for y, yl, ml in zip(ys, y_low, m_low)]
            ds = [
                1.5 * d - (0.5 * c) * mm - 0.5 * dot(ml, dl)
                for d, mm, ml, dl in zip(ds, ms, m_low, d_low)
            ]
            c = 1.5 * c
        y_low = [y.astype(BF) for y in ys]
        d_low = [d.astype(BF) for d in ds]
        xs = []
        if patches[0] == 0:
            for copy in tile_copies:
                copy.wait_recv()
        centers = {}
        for t in patches:
            tile = members[:, t].reshape(K, 128).astype(F32)
            centers[t] = jnp.sum(tile, axis=0, keepdims=True) * (1.0 / K)
            spread = tile - centers[t]
            pull = summed[:, t : t + 1] + summed[:, 4 + t : 5 + t]
            xs.append(jnp.concatenate([spread, jnp.broadcast_to(pull, (K, 128))], axis=1))
        gs = [c * x + dot(dl, x.astype(BF)) for x, dl in zip(xs, d_low)]
        hs = [dot(yl, g.astype(BF)) for yl, g in zip(y_low, gs)]
        gs = [
            1.5 * g - 0.5 * (c * h + dot(dl, h.astype(BF))) for g, h, dl in zip(gs, hs, d_low)
        ]
        for t, g, sc in zip(patches, gs, scale):
            shift = jnp.sum(g[:, 0:128] * g[:, 128:256], axis=0, keepdims=True) * sc
            final = centers[t] + shift + jnp.sqrt(float(K - 1) * sc) * g[:, 0:128]
            send_back[t // 2, :, t % 2] = final.astype(BF).reshape(NMEM, MEM_DEV, 128)

    back_copies = []
    for half in range(2):
        solve((2 * half, 2 * half + 1))
        copies = [
            exchange(d, send_back.at[half], back.at[half], back_send.at[half], back_recv.at[half])
            for d in range(1, NMEM)
        ]
        for copy in copies:
            copy.start()
        back[half, m] = send_back[half, m]
        back_copies.append(copies)

    order = cell_order(True)
    for p in range(2):
        for copy in back_copies[p]:
            copy.wait_recv()
        for half in range(2):
            tiles = [back[p, 4 * half + q // 2, q % 2].astype(F32) for q in range(8)]
            for c, channel in enumerate(block_swap(tiles)):
                rel_b[half, pl.ds(c, MEM_DEV, stride=C), :] = channel
        cells = jnp.concatenate([rel_b[0], rel_b[1]], axis=1).astype(BF)
        out_ref[:, 256 * p : 256 * p + 256] = dot(cells, order).astype(BF)

    @pl.when(r < NREG - 1)
    def _():
        halo_copy(True).wait_send()

    @pl.when(r > 0)
    def _():
        halo_copy(False).wait_send()

    for copy in rows_copies + seen_copies + tile_copies:
        copy.wait_send()
    for d in range(1, NMEM):

        @pl.when(middle(peer(d)))
        def _(d=d):
            side_copy(d).wait_send()

    for slot, (dr, dm) in enumerate(NEAR):
        if slot == 4:
            continue

        leaves = inside(dr, dm)
        if dr == 0:
            leaves = leaves & jnp.logical_not(crosses(dm))

        @pl.when(leaves)
        def _(slot=slot):
            near_copy(slot).wait_send()

    for copies in back_copies:
        for copy in copies:
            copy.wait_send()


def body(
    ensemble,
    conv_first,
    bias_first,
    conv_second,
    bias_second,
    observed_cell,
    observed_value,
    observed_precision,
):
    vmem = pl.BlockSpec(memory_space=pltpu.VMEM)
    rows = NPC * MEM_DEV
    result = pl.pallas_call(
        kernel,
        out_shape=jax.ShapeDtypeStruct((MEM_DEV * C, 512), BF),
        in_specs=[pl.BlockSpec(memory_space=pltpu.HBM)] * 8,
        out_specs=vmem,
        scratch_shapes=[
            pltpu.VMEM((MEM_DEV * C, 512), BF),
            pltpu.VMEM((2 * 9 * C, HID), BF),
            pltpu.VMEM((2, HID), F32),
            pltpu.VMEM((2 * 9 * C, HID), BF),
            pltpu.VMEM((2, C), F32),
            pltpu.VMEM((2, 2, 32), jnp.int32),
            pltpu.VMEM((2, 2, 32), F32),
            pltpu.VMEM((2, 2, 32), F32),
            pltpu.SemaphoreType.DMA((8,)),
            pltpu.VMEM((NMEM, 8, 128), F32),
            pltpu.VMEM((NMEM, 128, 128), BF),
            pltpu.VMEM((NMEM, MEM_DEV, 128), BF),
            pltpu.VMEM((NMEM, MEM_DEV, 128), BF),
            pltpu.VMEM((NMEM, MEM_DEV, 128), BF),
            pltpu.VMEM((24, 2, 2, 128, 128), F32),
            pltpu.VMEM((2, 6, 256, 256), BF),
            pltpu.VMEM((2, 6, 256, 256), BF),
            pltpu.VMEM((2, 4, NPC + 2, MEM_DEV, 128), BF),
            pltpu.VMEM((4, rows, 256), BF),
            pltpu.VMEM((4, 4, rows, 256), BF),
            pltpu.VMEM((2, 256, 128), F32),
            pltpu.VMEM((2, 256, 128), F32),
            pltpu.VMEM((NMEM, 4, MEM_DEV, 128), BF),
            pltpu.VMEM((NMEM, 4, MEM_DEV, 128), BF),
            pltpu.VMEM((9, K + 16, 128), BF),
            pltpu.VMEM((4, K, 9 * 128), BF),
            pltpu.VMEM((4, 16, 128), F32),
            pltpu.VMEM((2, NMEM, 2, MEM_DEV, 128), BF),
            pltpu.VMEM((2, NMEM, 2, MEM_DEV, 128), BF),
            pltpu.SemaphoreType.DMA((2,)),
            pltpu.SemaphoreType.DMA((2,)),
            pltpu.SemaphoreType.DMA((NMEM,)),
            pltpu.SemaphoreType.DMA((NMEM,)),
            pltpu.SemaphoreType.DMA((9,)),
            pltpu.SemaphoreType.DMA((9,)),
            pltpu.SemaphoreType.DMA((2, NMEM)),
            pltpu.SemaphoreType.DMA((2, NMEM)),
            pltpu.SemaphoreType.DMA((NMEM,)),
            pltpu.SemaphoreType.DMA((NMEM,)),
            pltpu.SemaphoreType.DMA((NMEM,)),
            pltpu.SemaphoreType.DMA((NMEM,)),
            pltpu.SemaphoreType.DMA((NMEM,)),
            pltpu.SemaphoreType.DMA((NMEM,)),
        ],
        compiler_params=pltpu.CompilerParams(
            collective_id=0, has_side_effects=True, vmem_limit_bytes=56 * 1024 * 1024
        ),
    )(
        ensemble.reshape(MEM_DEV * C, 512),
        conv_first.reshape(2 * 9 * C, HID),
        bias_first,
        conv_second.transpose(0, 1, 3, 2).reshape(2 * 9 * C, HID),
        bias_second,
        observed_cell,
        observed_value,
        observed_precision,
    )
    return result.reshape(MEM_DEV, C, 512)


def solution(mesh):
    in_specs = (
        P("mem", None, "reg"),
        P(),
        P(),
        P(),
        P(),
        P("reg", "mem", None),
        P("reg", "mem", None),
        P("reg", "mem", None),
    )
    out_specs = P("mem", None, "reg")
    return jax.shard_map(body, mesh=mesh, in_specs=in_specs, out_specs=out_specs, check_vma=False)
```

```python
import jax
import jax.numpy as jnp
from jax import lax
from jax.experimental import pallas as pl
from jax.experimental.pallas import tpu as pltpu
from jax.sharding import PartitionSpec as P

K = 256
C = 8
HID = 64
NMEM = 8
NREG = 32
MEM_DEV = 32
NPC = 16
BF = jnp.bfloat16
F32 = jnp.float32
NEAR = [(dr, dm) for dr in (-1, 0, 1) for dm in (-1, 0, 1)]
TOP, BOTTOM = 4, 5


def dot(a, b):
    return lax.dot_general(a, b, (((1,), (0,)), ((), ())), preferred_element_type=F32)


def dot_nt(a, b):
    return lax.dot_general(a, b, (((1,), (1,)), ((), ())), preferred_element_type=F32)


def iota(shape, dim):
    return lax.broadcasted_iota(jnp.int32, shape, dim)


def block_swap(arrays):
    block = iota(arrays[0].shape, 1) // 16
    for step in (1, 2, 4):
        high = (block & step) != 0
        swapped = list(arrays)
        for a in range(8):
            if a & step:
                continue
            b = a | step
            swapped[a] = jnp.where(high, pltpu.roll(arrays[b], 16 * step, 1), arrays[a])
            swapped[b] = jnp.where(high, arrays[b], pltpu.roll(arrays[a], 128 - 16 * step, 1))
        arrays = swapped
    return arrays


def cell_order(inverse):
    plain, tiled = iota((256, 256), 1 if inverse else 0), iota((256, 256), 0 if inverse else 1)
    source = ((tiled // 4) % 4) * 64 + (tiled // 16) * 4 + tiled % 4
    return jnp.where(plain == source, 1.0, 0.0).astype(BF)


def strips_of(taps, flip):
    zero = jnp.zeros((C, HID), F32)
    strips = {}
    for row_step in (-1, 0, 1):
        for col in range(-1, 5):
            pieces = []
            for j in range(4):
                step = j - col if flip else col - j
                pieces.append(taps[3 * (row_step + 1) + step + 1] if abs(step) <= 1 else zero)
            strips[row_step, col] = jnp.concatenate(pieces, axis=1)
    return strips


def build_weights(taps, flip, raw, base):
    strips = strips_of(taps, flip)
    for tile in range(6):
        for row in range(4):
            if flip:
                hidden_row = {TOP: -1, BOTTOM: 4}.get(tile, tile)
                step = hidden_row - row
            else:
                step = {TOP: row - 4, BOTTOM: row + 4 - 3}.get(tile, row - tile)
            if abs(step) > 1:
                continue
            for side in (0, 1):
                for j in range(4):
                    col = j
                    if side:
                        col = {0: 4, 3: -1}.get(j)
                    if col is None:
                        continue
                    rows = pl.ds(4 * row + j, C, stride=16)
                    raw[base + tile, side, 0, rows, :] = strips[step, col][:, 0:128]
                    raw[base + tile, side, 1, rows, :] = strips[step, col][:, 128:256]


def kernel(
    ens_hbm,
    first_hbm,
    bias_a_hbm,
    second_hbm,
    bias_b_hbm,
    cell_hbm,
    value_hbm,
    prec_hbm,
    out_ref,
    ens_ref,
    first_ref,
    bias_a_ref,
    second_ref,
    bias_b_ref,
    cell_ref,
    value_ref,
    prec_ref,
    load_sem,
    rows_of,
    picker,
    seen_send,
    seen_all,
    seen_side,
    raw,
    w_a,
    w_b,
    field,
    wide,
    hid,
    ahead,
    rel,
    rel_b,
    send_tiles,
    members,
    near,
    local,
    decay,
    send_back,
    back,
    halo_send,
    halo_recv,
    tile_send,
    tile_recv,
    near_send,
    near_recv,
    back_send,
    back_recv,
    rows_send,
    rows_recv,
    seen_send_sem,
    seen_recv_sem,
    side_send,
    side_recv,
):
    m = lax.axis_index("mem")
    r = lax.axis_index("reg")
    barrier = pltpu.get_barrier_semaphore()

    def inside(dr, dm):
        return (r + dr >= 0) & (r + dr < NREG) & (m + dm >= 0) & (m + dm < NMEM)

    def peer(d):
        return lax.rem(m + d, NMEM)

    def middle(index):
        return (index == NMEM // 2 - 1) | (index == NMEM // 2)

    def crosses(dm):
        if dm == 0:
            return jnp.bool_(False)
        return m == (NMEM // 2 - 1 if dm > 0 else NMEM // 2)

    for d in range(1, NMEM):
        pl.semaphore_signal(
            barrier, inc=1, device_id={"mem": peer(d), "reg": r}, device_id_type=pl.DeviceIdType.MESH
        )
    arrivals = jnp.int32(NMEM - 1)
    for dr, dm in NEAR:
        if dr == 0:
            continue

        @pl.when(inside(dr, dm))
        def _(dr=dr, dm=dm):
            pl.semaphore_signal(
                barrier,
                inc=1,
                device_id={"mem": m + dm, "reg": r + dr},
                device_id_type=pl.DeviceIdType.MESH,
            )

        arrivals = arrivals + jnp.where(inside(dr, dm), 1, 0)

    loads = [
        pltpu.make_async_copy(source, target, load_sem.at[i])
        for i, (source, target) in enumerate(
            (
                (ens_hbm, ens_ref),
                (first_hbm, first_ref),
                (bias_a_hbm, bias_a_ref),
                (second_hbm, second_ref),
                (bias_b_hbm, bias_b_ref),
                (cell_hbm, cell_ref),
                (value_hbm, value_ref),
                (prec_hbm, prec_ref),
            )
        )
    ]
    for load in loads:
        load.start()

    order = cell_order(False)
    loads[0].wait()
    for p in range(2):
        cells = dot(ens_ref[:, 256 * p : 256 * p + 256], order)
        rel[0] = cells[:, 0:128]
        rel[1] = cells[:, 128:256]
        for half in range(2):
            channels = [rel[half, pl.ds(c, MEM_DEV, stride=C), :] for c in range(C)]
            for q, tile in enumerate(block_swap(channels)):
                field[0, 1 + p, 1 + 8 * half + q] = tile.astype(BF)
    pl.semaphore_wait(barrier, arrivals)

    def exchange(d, source, target, send_sem, recv_sem, own=None):
        return pltpu.make_async_remote_copy(
            src_ref=source.at[peer(d) if own is None else own],
            dst_ref=target.at[m],
            send_sem=send_sem.at[d],
            recv_sem=recv_sem.at[d],
            device_id={"mem": peer(d), "reg": r},
            device_id_type=pl.DeviceIdType.MESH,
        )

    def halo_copy(down):
        return pltpu.make_async_remote_copy(
            src_ref=field.at[0, 2 if down else 1, pl.ds(1, NPC)],
            dst_ref=field.at[0, 0 if down else 3, pl.ds(1, NPC)],
            send_sem=halo_send.at[1 if down else 0],
            recv_sem=halo_recv.at[1 if down else 0],
            device_id={"mem": m, "reg": r + 1 if down else r - 1},
            device_id_type=pl.DeviceIdType.MESH,
        )

    @pl.when(r < NREG - 1)
    def _():
        halo_copy(True).start()

    @pl.when(r > 0)
    def _():
        halo_copy(False).start()

    edge = jnp.zeros((MEM_DEV, 128), BF)
    for f in range(2):
        for p in range(4):
            field[f, p, 0] = edge
            field[f, p, NPC + 1] = edge

    @pl.when(r == 0)
    def _():
        field[0, 0, 1 : NPC + 1] = jnp.zeros((NPC, MEM_DEV, 128), BF)

    @pl.when(r == NREG - 1)
    def _():
        field[0, 3, 1 : NPC + 1] = jnp.zeros((NPC, MEM_DEV, 128), BF)

    for slot, (dr, dm) in enumerate(NEAR):
        if (dr, dm) == (0, 0):
            continue

        @pl.when(jnp.logical_not(inside(dr, dm)))
        def _(slot=slot):
            near[slot] = jnp.zeros((K + 16, 128), BF)

    for load in loads[1:]:
        load.wait()

    def row_of(ref):
        return jnp.concatenate([ref[t // 2, t % 2 : t % 2 + 1, :] for t in range(4)], axis=1)

    rows_of[m] = jnp.concatenate(
        [row_of(cell_ref).astype(F32), row_of(value_ref), row_of(prec_ref), jnp.zeros((5, 128), F32)],
        axis=0,
    )

    rows_copies = [exchange(d, rows_of, rows_of, rows_send, rows_recv, m) for d in range(1, NMEM)]
    for copy in rows_copies:
        copy.start()

    raw[...] = jnp.zeros(raw.shape, F32)
    for f in range(2):
        taps = [
            0.5 * first_ref[pl.ds((9 * f + t) * C, C), :].astype(F32) for t in range(9)
        ]
        build_weights(taps, False, raw, 12 * f)
        taps = [second_ref[pl.ds((9 * f + t) * C, C), :].astype(F32) for t in range(9)]
        build_weights(taps, True, raw, 12 * f + 6)
        for tile in range(6):
            for side in range(2):
                span = slice(128 * side, 128 * side + 128)
                for part in range(2):
                    lanes = slice(128 * part, 128 * part + 128)
                    w_a[f, tile, span, lanes] = raw[12 * f + tile, side, part].astype(BF)
                    w_b[f, tile, lanes, span] = jnp.transpose(
                        raw[12 * f + 6 + tile, side, part]
                    ).astype(BF)

    lane = iota((1, 128), 1)
    for target in range(4):
        for slot, (dr, dm) in enumerate(NEAR):
            a = 2 * dr + lane // 64 - target // 2
            b = 2 * dm + (lane // 32) % 2 - target % 2
            keep = (jnp.abs(a) <= 2) & (jnp.abs(b) <= 2) & inside(dr, dm)
            fall = jnp.exp((a * a + b * b).astype(F32) * (-1.0 / 9.0))
            decay[target, slot : slot + 1, :] = jnp.where(keep, fall, 0.0)

    row_lane = iota((1, 1, 128), 2)
    bias_lane = iota((1, 128), 1)
    keep_top = jnp.where(r == 0, 0.0, 1.0).astype(F32)
    keep_bottom = jnp.where(r == NREG - 1, 0.0, 1.0).astype(F32)
    keep = (keep_top, None, None, keep_bottom)

    def widen(f, p):
        right = field[f, p, 2 : NPC + 2].astype(F32)
        left = field[f, p, 0:NPC].astype(F32)
        side = jnp.where(row_lane % 4 < 2, right, left).astype(BF)
        wide[p, :, 0:128] = field[f, p, 1 : NPC + 1].reshape(NPC * MEM_DEV, 128)
        wide[p, :, 128:256] = side.reshape(NPC * MEM_DEV, 128)

    def hidden(f, p, i, bias):
        total = dot(wide[p], w_a[f, i])
        if i == 0:
            total = total + dot(wide[p - 1], w_a[f, TOP])
        if i == 3:
            total = total + dot(wide[p + 1], w_a[f, BOTTOM])
        total = total + bias
        total = total + total * jnp.tanh(total)
        if keep[p] is not None:
            total = total * keep[p]
        hid[p, i] = total.astype(BF)

    def branch(f, p, bias):
        total = None
        terms = [(p, i, i) for i in range(4)] + [(p - 1, 3, TOP), (p + 1, 0, BOTTOM)]
        if f == 0 and p in (1, 2):
            total = ahead[p - 1]
            terms = [(1, 0, 0), (0, 3, TOP)] if p == 1 else [(2, 3, 3), (3, 0, BOTTOM)]
        if p == 0:
            terms = [(0, 1, 1), (0, 2, 2), (0, 3, 3), (1, 0, BOTTOM)]
        if p == 3:
            terms = [(3, 0, 0), (3, 1, 1), (3, 2, 2), (2, 3, TOP)]
        for hp, hi, tile in terms:
            part = dot(hid[hp, hi], w_b[f, tile])
            total = part if total is None else total + part
        own = total[:, 0:128].reshape(NPC, MEM_DEV, 128)
        side = total[:, 128:256].reshape(NPC, MEM_DEV, 128)
        none = jnp.zeros((1, MEM_DEV, 128), F32)
        before = jnp.concatenate([none, side[: NPC - 1]], axis=0)
        after = jnp.concatenate([side[1:], none], axis=0)
        moved = jnp.where(row_lane % 4 < 2, before, after)
        result = field[f, p, 1 : NPC + 1].astype(F32) + (own + moved + bias[None])
        if keep[p] is not None:
            result = result * keep[p]
        return result.astype(BF)

    def biases(f):
        half = 0.5 * bias_a_ref[f : f + 1, :]
        first = jnp.concatenate([half] * 4, axis=1)
        second = jnp.zeros((1, 128), F32)
        for c in range(C):
            second = jnp.where(bias_lane // 16 == c, bias_b_ref[f : f + 1, c : c + 1], second)
        return first, second

    bias_a, bias_b = biases(0)
    widen(0, 1)
    widen(0, 2)
    for p, i in ((1, 1), (1, 2), (2, 1), (2, 2), (1, 3), (2, 0)):
        hidden(0, p, i, bias_a)
    for p, terms in (
        (1, [(1, 1, 1), (1, 2, 2), (1, 3, 3), (2, 0, BOTTOM)]),
        (2, [(2, 0, 0), (2, 1, 1), (2, 2, 2), (1, 3, TOP)]),
    ):
        total = None
        for hp, hi, tile in terms:
            part = dot(hid[hp, hi], w_b[0, tile])
            total = part if total is None else total + part
        ahead[p - 1] = total

    @pl.when(r < NREG - 1)
    def _():
        halo_copy(False).wait_recv()

    @pl.when(r > 0)
    def _():
        halo_copy(True).wait_recv()

    widen(0, 0)
    widen(0, 3)
    for p, i in ((1, 0), (2, 3), (0, 1), (0, 2), (0, 3), (3, 0), (3, 1), (3, 2)):
        hidden(0, p, i, bias_a)
    for p in range(4):
        field[1, p, 1 : NPC + 1] = branch(0, p, bias_b)

    for copy in rows_copies:
        copy.wait_recv()
    for b in range(NMEM):
        cells = rows_of[b, 0:1, :]
        picker[b] = jnp.where(iota((128, 128), 0).astype(F32) == cells, 1.0, 0.0).astype(BF)

    bias_a, bias_b = biases(1)
    for p in range(4):
        widen(1, p)
    hidden(1, 0, 3, bias_a)
    hidden(1, 3, 0, bias_a)
    for p in (1, 2):
        for i in range(4):
            hidden(1, p, i, bias_a)
    for p in (1, 2):
        tiles = branch(1, p, bias_b).reshape(NMEM, 2, MEM_DEV, 128)
        for ql in range(2):
            send_tiles[p - 1, :, ql] = tiles[:, ql]

    for b in range(NMEM):
        found = dot(send_tiles[:, b].reshape(4 * MEM_DEV, 128), picker[b])
        seen = found[0:MEM_DEV]
        for t in range(1, 4):
            seen = jnp.where(lane // 32 == t, found[MEM_DEV * t : MEM_DEV * t + MEM_DEV], seen)
        seen_send[b] = seen.astype(BF)

    def side_copy(d):
        return pltpu.make_async_remote_copy(
            src_ref=seen_send.at[NMEM - 1 - peer(d)],
            dst_ref=seen_side.at[m],
            send_sem=side_send.at[d],
            recv_sem=side_recv.at[d],
            device_id={"mem": peer(d), "reg": r},
            device_id_type=pl.DeviceIdType.MESH,
        )

    seen_copies = [
        exchange(d, seen_send, seen_all, seen_send_sem, seen_recv_sem) for d in range(1, NMEM)
    ]
    for copy in seen_copies:
        copy.start()
    for d in range(1, NMEM):

        @pl.when(middle(peer(d)))
        def _(d=d):
            side_copy(d).start()

    def tile_half(half):
        return [
            exchange(
                d, send_tiles.at[half], members.at[half], tile_send.at[half], tile_recv.at[half]
            )
            for d in range(1, NMEM)
        ]

    tile_copies = [tile_half(0), tile_half(1)]
    for copy in tile_copies[0] + tile_copies[1]:
        copy.start()
    members[:, m] = send_tiles[:, m]

    seen_all[m] = seen_send[m]
    for copy in seen_copies:
        copy.wait_recv()

    def anomalies(values, owner, slot):
        seen = values[...].reshape(K, 128).astype(F32)
        center = jnp.sum(seen, axis=0, keepdims=True) * (1.0 / K)
        root = jnp.sqrt(rows_of[owner, 2:3, :])
        near[slot, 0:K] = ((seen - center) * root).astype(BF)
        depart = (rows_of[owner, 1:2, :] - center) * root
        high = depart.astype(BF).astype(F32)
        sub = iota((16, 128), 0)
        near[slot, K : K + 16] = jnp.where(
            sub == 0, high, jnp.where(sub == 1, depart - high, 0.0)
        ).astype(BF)

    anomalies(seen_all, m, 4)

    def near_copy(slot):
        dr, dm = NEAR[slot]
        return pltpu.make_async_remote_copy(
            src_ref=near.at[4],
            dst_ref=near.at[8 - slot],
            send_sem=near_send.at[slot],
            recv_sem=near_recv.at[8 - slot],
            device_id={"mem": m + dm, "reg": r + dr},
            device_id_type=pl.DeviceIdType.MESH,
        )

    for slot in (0, 2, 6, 8, 1, 7, 3, 5):
        dr, dm = NEAR[slot]

        @pl.when(inside(dr, dm) & jnp.logical_not(crosses(dm)))
        def _(slot=slot):
            near_copy(slot).start()

    def cross_copy(dr, dm):
        return pltpu.make_async_remote_copy(
            src_ref=near.at[4 + dm],
            dst_ref=near.at[3 * (1 - dr) + 1 + dm],
            send_sem=near_send.at[3 * (1 + dr) + 1 + dm],
            recv_sem=near_recv.at[3 * (1 - dr) + 1 + dm],
            device_id={"mem": m, "reg": r + dr},
            device_id_type=pl.DeviceIdType.MESH,
        )

    for dm in (-1, 1):

        @pl.when(crosses(dm))
        def _(dm=dm):
            seen_side[m] = seen_send[NMEM - 1 - m]
            for d in range(1, NMEM):
                side_copy(d).wait_recv()
            anomalies(seen_side, NMEM - 1 - m, 4 + dm)

        for dr in (-1, 1):

            @pl.when(crosses(dm) & inside(dr, dm))
            def _(dr=dr, dm=dm):
                cross_copy(dr, dm).start()

    summed = jnp.zeros((K, 8), F32)
    for slot in (4, 3, 5, 1, 7, 0, 2, 6, 8):
        dr, dm = NEAR[slot]
        if slot != 4:
            arrives = inside(dr, dm)
            if dr == 0:
                arrives = arrives & jnp.logical_not(crosses(dm))

            @pl.when(arrives)
            def _(slot=slot):
                near_copy(8 - slot).wait_recv()

        block = near[slot, 0:K].astype(F32)
        tail = near[slot, K : K + 16].astype(F32)
        depart = tail[0:1] + tail[1:2]
        pulls = []
        for t in range(4):
            fall = decay[t, slot : slot + 1, :]
            local[t, :, 128 * slot : 128 * slot + 128] = (block * fall).astype(BF)
            pulls.append(fall * fall * depart)
        pulls = jnp.concatenate(pulls, axis=0)
        high = pulls.astype(BF).astype(F32)
        both = jnp.concatenate([high, pulls - high], axis=0).astype(BF)
        summed = summed + dot_nt(near[slot, 0:K], both)

    eye = jnp.where(iota((K, K), 0) == iota((K, K), 1), float(K - 1), 0.0)

    def solve(patches):
        scale, ys, ds = [], [], []
        for t in patches:
            system = dot_nt(local[t], local[t]) + eye
            rows = jnp.sum(jnp.abs(system), axis=0, keepdims=True)
            scale.append(1.0 / jnp.max(rows, axis=1, keepdims=True))
            ds.append(system * scale[-1])
        lows = [a.astype(BF) for a in ds]
        ys = [1.5 * a - 0.5 * dot(low, low) for a, low in zip(ds, lows)]
        ds = [-0.5 * a for a in ds]
        c = 1.5
        for _ in range(2):
            y_low = [y.astype(BF) for y in ys]
            d_low = [d.astype(BF) for d in ds]
            ms = [c * y + dot(dl, yl) for y, dl, yl in zip(ys, d_low, y_low)]
            m_low = [mm.astype(BF) for mm in ms]
            ys = [1.5 * y - 0.5 * dot(yl, ml) for y, yl, ml in zip(ys, y_low, m_low)]
            ds = [
                1.5 * d - (0.5 * c) * mm - 0.5 * dot(ml, dl)
                for d, mm, ml, dl in zip(ds, ms, m_low, d_low)
            ]
            c = 1.5 * c
        y_low = [y.astype(BF) for y in ys]
        d_low = [d.astype(BF) for d in ds]
        xs = []
        for copy in tile_copies[patches[0] // 2]:
            copy.wait_recv()
        centers = {}
        for t in patches:
            tile = members[t // 2, :, t % 2].reshape(K, 128).astype(F32)
            centers[t] = jnp.sum(tile, axis=0, keepdims=True) * (1.0 / K)
            spread = tile - centers[t]
            pull = summed[:, t : t + 1] + summed[:, 4 + t : 5 + t]
            xs.append(jnp.concatenate([spread, jnp.broadcast_to(pull, (K, 128))], axis=1))
        gs = [c * x + dot(dl, x.astype(BF)) for x, dl in zip(xs, d_low)]
        hs = [dot(yl, g.astype(BF)) for yl, g in zip(y_low, gs)]
        gs = [
            1.5 * g - 0.5 * (c * h + dot(dl, h.astype(BF))) for g, h, dl in zip(gs, hs, d_low)
        ]
        for t, g, sc in zip(patches, gs, scale):
            shift = jnp.sum(g[:, 0:128] * g[:, 128:256], axis=0, keepdims=True) * sc
            final = centers[t] + shift + jnp.sqrt(float(K - 1) * sc) * g[:, 0:128]
            send_back[t // 2, :, t % 2] = final.astype(BF).reshape(NMEM, MEM_DEV, 128)

    back_copies = []
    for half in range(2):
        solve((2 * half, 2 * half + 1))
        copies = [
            exchange(d, send_back.at[half], back.at[half], back_send.at[half], back_recv.at[half])
            for d in range(1, NMEM)
        ]
        for copy in copies:
            copy.start()
        back[half, m] = send_back[half, m]
        back_copies.append(copies)

    order = cell_order(True)
    for p in range(2):
        for copy in back_copies[p]:
            copy.wait_recv()
        for half in range(2):
            tiles = [back[p, 4 * half + q // 2, q % 2].astype(F32) for q in range(8)]
            for c, channel in enumerate(block_swap(tiles)):
                rel_b[half, pl.ds(c, MEM_DEV, stride=C), :] = channel
        cells = jnp.concatenate([rel_b[0], rel_b[1]], axis=1).astype(BF)
        out_ref[:, 256 * p : 256 * p + 256] = dot(cells, order).astype(BF)

    @pl.when(r < NREG - 1)
    def _():
        halo_copy(True).wait_send()

    @pl.when(r > 0)
    def _():
        halo_copy(False).wait_send()

    for copy in rows_copies + seen_copies + tile_copies[0] + tile_copies[1]:
        copy.wait_send()
    for d in range(1, NMEM):

        @pl.when(middle(peer(d)))
        def _(d=d):
            side_copy(d).wait_send()

    for slot, (dr, dm) in enumerate(NEAR):
        if slot == 4:
            continue

        leaves = inside(dr, dm)
        if dr == 0:
            leaves = leaves & jnp.logical_not(crosses(dm))

        @pl.when(leaves)
        def _(slot=slot):
            near_copy(slot).wait_send()

    for copies in back_copies:
        for copy in copies:
            copy.wait_send()


def body(
    ensemble,
    conv_first,
    bias_first,
    conv_second,
    bias_second,
    observed_cell,
    observed_value,
    observed_precision,
):
    vmem = pl.BlockSpec(memory_space=pltpu.VMEM)
    rows = NPC * MEM_DEV
    result = pl.pallas_call(
        kernel,
        out_shape=jax.ShapeDtypeStruct((MEM_DEV * C, 512), BF),
        in_specs=[pl.BlockSpec(memory_space=pltpu.HBM)] * 8,
        out_specs=vmem,
        scratch_shapes=[
            pltpu.VMEM((MEM_DEV * C, 512), BF),
            pltpu.VMEM((2 * 9 * C, HID), BF),
            pltpu.VMEM((2, HID), F32),
            pltpu.VMEM((2 * 9 * C, HID), BF),
            pltpu.VMEM((2, C), F32),
            pltpu.VMEM((2, 2, 32), jnp.int32),
            pltpu.VMEM((2, 2, 32), F32),
            pltpu.VMEM((2, 2, 32), F32),
            pltpu.SemaphoreType.DMA((8,)),
            pltpu.VMEM((NMEM, 8, 128), F32),
            pltpu.VMEM((NMEM, 128, 128), BF),
            pltpu.VMEM((NMEM, MEM_DEV, 128), BF),
            pltpu.VMEM((NMEM, MEM_DEV, 128), BF),
            pltpu.VMEM((NMEM, MEM_DEV, 128), BF),
            pltpu.VMEM((24, 2, 2, 128, 128), F32),
            pltpu.VMEM((2, 6, 256, 256), BF),
            pltpu.VMEM((2, 6, 256, 256), BF),
            pltpu.VMEM((2, 4, NPC + 2, MEM_DEV, 128), BF),
            pltpu.VMEM((4, rows, 256), BF),
            pltpu.VMEM((4, 4, rows, 256), BF),
            pltpu.VMEM((2, rows, 256), F32),
            pltpu.VMEM((2, 256, 128), F32),
            pltpu.VMEM((2, 256, 128), F32),
            pltpu.VMEM((2, NMEM, 2, MEM_DEV, 128), BF),
            pltpu.VMEM((2, NMEM, 2, MEM_DEV, 128), BF),
            pltpu.VMEM((9, K + 16, 128), BF),
            pltpu.VMEM((4, K, 9 * 128), BF),
            pltpu.VMEM((4, 16, 128), F32),
            pltpu.VMEM((2, NMEM, 2, MEM_DEV, 128), BF),
            pltpu.VMEM((2, NMEM, 2, MEM_DEV, 128), BF),
            pltpu.SemaphoreType.DMA((2,)),
            pltpu.SemaphoreType.DMA((2,)),
            pltpu.SemaphoreType.DMA((2, NMEM)),
            pltpu.SemaphoreType.DMA((2, NMEM)),
            pltpu.SemaphoreType.DMA((9,)),
            pltpu.SemaphoreType.DMA((9,)),
            pltpu.SemaphoreType.DMA((2, NMEM)),
            pltpu.SemaphoreType.DMA((2, NMEM)),
            pltpu.SemaphoreType.DMA((NMEM,)),
            pltpu.SemaphoreType.DMA((NMEM,)),
            pltpu.SemaphoreType.DMA((NMEM,)),
            pltpu.SemaphoreType.DMA((NMEM,)),
            pltpu.SemaphoreType.DMA((NMEM,)),
            pltpu.SemaphoreType.DMA((NMEM,)),
        ],
        compiler_params=pltpu.CompilerParams(
            collective_id=0, has_side_effects=True, vmem_limit_bytes=56 * 1024 * 1024
        ),
    )(
        ensemble.reshape(MEM_DEV * C, 512),
        conv_first.reshape(2 * 9 * C, HID),
        bias_first,
        conv_second.transpose(0, 1, 3, 2).reshape(2 * 9 * C, HID),
        bias_second,
        observed_cell,
        observed_value,
        observed_precision,
    )
    return result.reshape(MEM_DEV, C, 512)


def solution(mesh):
    in_specs = (
        P("mem", None, "reg"),
        P(),
        P(),
        P(),
        P(),
        P("reg", "mem", None),
        P("reg", "mem", None),
        P("reg", "mem", None),
    )
    out_specs = P("mem", None, "reg")
    return jax.shard_map(body, mesh=mesh, in_specs=in_specs, out_specs=out_specs, check_vma=False)
```
